128 devices in a mesh: row: 16 (over z, y), col: 8 (over x, core).
Axes of the slice: x: 4, y: 4, z: 4, core: 2. Of those that a mesh axis runs over, the one named last changes fastest.
Arguments:
- front: bfloat16 [32768, 32768], P('row', 'col'), may hold values from -0.0625 to 0.0625
- tile_mask: int32 [128, 128], P('row', 'col'), may hold values 0 or 1
- probes: bfloat16 [32768, 256], P(('col', 'row')), may hold values from -6 to 6
- coupling: float32 [32768, 256], P(('row', 'col')), may hold values from -0.375 to 0.375
Outputs:
- leaf_basis: float32 [32768, 256], P(('row', 'col'))
- upper_transfer: float32 [6, 32768, 256], P(None, ('row', 'col'))
The draws below stay inside these ranges and needn't reach their ends.
Inputs may be any that keep to these rules, and one draw needn't show every extreme that they name: `tile_mask`: 1 where a tile of the front is present, 0 where it is absent.
All inputs are finite; a program needn't handle non-finite values. No bound on the sum of `tile_mask` on one device may be relied on, other than what follows from the above.
Results may differ from the reference program's by a relative error of at most 0.0003.
Values may be sent and summed in bfloat16 or wider, within the bound.
A program may use at most 128 MiB of HBM per device.

```python
import jax
import jax.numpy as jnp
from jax import lax

LEAF = 256
PROBES = 256
LEAVES = 128
FRONT = 32768
LEVELS = 7


def place_ends(entries, own_key, least, largest):
    place = [jax.random.randint(jax.random.fold_in(own_key, axis), (), 0, length) for axis, length in enumerate(entries.shape)]
    longest = entries.shape.index(max(entries.shape))
    neighbour = place[:longest] + [(place[longest] + 1) % entries.shape[longest]] + place[longest + 1:]
    return entries.at[tuple(place)].set(least).at[tuple(neighbour)].set(largest)


def steps_of(own_key, shape, pieces, low, largest):
    level, own = 1.0, jax.random.fold_in(own_key, 6)
    for axis_at, shards_of in pieces:
        steps = jnp.exp(jax.random.uniform(jax.random.fold_in(own, axis_at), (shards_of,), jnp.float32, low / len(pieces), largest / len(pieces)))
        level = level * jnp.repeat(steps, shape[axis_at] // shards_of).reshape([-1 if axis == axis_at else 1 for axis in range(len(shape))])
    return level


def scatter_about(key, extent, scale, limit, split=(), held_as=jnp.bfloat16):
    values = jax.random.normal(key, extent, jnp.float32) * scale
    if len(split) > 0:
        values = steps_of(key, extent, split, -0.22, 0.18) * values
    return jnp.clip(values, min=-limit, max=limit).astype(held_as)


def setup_inputs(seed: int = 0) -> dict:
    arg_keys = jax.random.split(jax.random.key(seed), 5)
    front = scatter_about(arg_keys[0], (FRONT, FRONT), (FRONT // 4) ** -0.5, 0.0625, ((0, 16), (1, 8)))
    tile_mask = place_ends((jax.random.randint(arg_keys[1], (LEAVES, LEAVES), 0, 4) < 1).astype(jnp.int32), jax.random.fold_in(arg_keys[1], 1), 0, 1)
    probes = scatter_about(arg_keys[2], (FRONT, PROBES), 1.0, 6.0, ((0, 128),))
    coupling = scatter_about(arg_keys[3], (LEAVES * PROBES, PROBES), PROBES ** -0.5, 0.375, ((0, 128),), jnp.float32)
    return dict(front=front, tile_mask=tile_mask, probes=probes, coupling=coupling)


def matmul_high(left, right):
    return jnp.matmul(left, right, precision=lax.Precision.HIGHEST)

def transpose_last(array):
    return jnp.swapaxes(array, -1, -2)

def merge_pair(top_node, bottom_node, level_index):
    top_s, top_w, top_p = top_node
    bottom_s, bottom_w, bottom_p = bottom_node
    if level_index > 1:
        factor = 2.0 ** (-(level_index - 1) / 2.0)
        top_s = top_s - factor * matmul_high(top_p, bottom_w)
        bottom_s = bottom_s - factor * matmul_high(bottom_p, top_w)
    stacked = jnp.concatenate([top_s, bottom_s], axis=-2)
    gram_matrix = matmul_high(transpose_last(stacked), stacked)
    probe_count = gram_matrix.shape[-1]
    shift_value = 0.001 * (jnp.trace(gram_matrix, axis1=-2, axis2=-1) / probe_count + 1e-06)
    gram_matrix = gram_matrix + shift_value[..., None, None] * jnp.eye(probe_count, dtype=jnp.float32)
    lower_factor = jnp.linalg.cholesky(gram_matrix)
    basis_rows = jax.scipy.linalg.solve_triangular(lower_factor, transpose_last(stacked), lower=True)
    new_w = matmul_high(basis_rows, jnp.concatenate([top_w, bottom_w], axis=-2))
    row_total = top_s.shape[-2]
    top_half = transpose_last(basis_rows[..., :row_total])
    bottom_half = transpose_last(basis_rows[..., row_total:])
    return ((transpose_last(lower_factor), new_w, top_p + bottom_p), top_half, bottom_half)

def reference(front, tile_mask, probes, coupling):
    tile_rows = jnp.arange(LEAVES, dtype=jnp.int32)
    pair_keep = (tile_rows[:, None] // 2 != tile_rows[None, :] // 2).astype(jnp.float32)
    keep_tiles = tile_mask.astype(jnp.float32) * pair_keep
    probe_full = probes.astype(jnp.float32)

    def row_block(tile_index):
        rows = lax.dynamic_slice_in_dim(front, tile_index * LEAF, LEAF, 0).astype(jnp.float32)
        weights = lax.dynamic_index_in_dim(keep_tiles, tile_index, 0, keepdims=False)
        rows = (rows.reshape(LEAF, LEAVES, LEAF) * weights[None, :, None]).reshape(LEAF, FRONT)
        return jnp.dot(rows, probe_full, precision=lax.Precision.HIGHEST)
    samples = lax.map(row_block, jnp.arange(LEAVES, dtype=jnp.int32))
    node_state = (samples, probe_full.reshape(LEAVES, LEAF, PROBES), coupling.reshape(LEAVES, PROBES, PROBES))
    leaf_basis = None
    uppers = []
    for level_index in range(1, LEVELS + 1):
        node_count = node_state[0].shape[0]
        paired = tuple((array.reshape((node_count // 2, 2) + array.shape[1:]) for array in node_state))
        node_state, top_half, bottom_half = merge_pair(tuple((array[:, 0] for array in paired)), tuple((array[:, 1] for array in paired)), level_index)
        children = jnp.stack([top_half, bottom_half], axis=1).reshape((node_count,) + top_half.shape[1:])
        if level_index == 1:
            leaf_basis = children.reshape(FRONT, PROBES)
        else:
            spread = jnp.repeat(children, 2 ** (level_index - 1), axis=0)
            uppers.append(spread.reshape(LEAVES * PROBES, PROBES))
    return (leaf_basis, jnp.stack(uppers, axis=0))
```

```python
import jax
import jax.numpy as jnp
from jax import lax
from jax.experimental import pallas as pl
from jax.experimental.pallas import tpu as pltpu
from jax.sharding import PartitionSpec as P

F32=jnp.float32; BF=jnp.bfloat16

def split(x):
    h=x.astype(BF); l=(x-h.astype(F32)).astype(BF); return h,l
def dg(a,b,dims):
    return lax.dot_general(a,b,(dims,((),())),preferred_element_type=F32)
NN=((1,),(0,)); NT=((1,),(1,)); TN=((0,),(0,))
def dot3(a,b,dims=NN):
    ah,al=a if isinstance(a,tuple) else split(a)
    bh,bl=b if isinstance(b,tuple) else split(b)
    return dg(ah,bh,dims)+(dg(ah,bl,dims)+dg(al,bh,dims))

def lanes(v,c): return jnp.broadcast_to(v[:,c:c+1],(8,128))
def subs(v,i): return jnp.broadcast_to(v[i:i+1,:],(8,128))

def factor64(E,off):
    sub=lax.broadcasted_iota(jnp.int32,(8,128),0)
    E=list(E); X=[]
    for p in range(8):
        row=[subs(E[p],i) for i in range(8)]
        a={}
        for i in range(8):
            for j in range(i,8):
                a[i,j]=lanes(row[i],off+8*p+j)
        V={}
        for n in range(p+1,8):
            V[n]=[lanes(E[n],off+8*p+k) for k in range(8)]
        out=[None]*8
        for m in range(4):
            P,Q=2*m,2*m+1
            aa,bb,cc=a[P,P],a[P,Q],a[Q,Q]
            det=aa*cc-bb*bb
            r=1.0/det
            ra=cc*r; rb=bb*r; rc=aa*r
            yp=ra*row[P]-rb*row[Q]
            yq=rc*row[Q]-rb*row[P]
            t={}
            for i in range(Q+1,8):
                u,v=a[P,i],a[Q,i]
                tp=(cc*u-bb*v)*r
                tq=(aa*v-bb*u)*r
                t[i]=(tp,tq)
                for j in range(i,8):
                    a[i,j]=a[i,j]-(tp*a[P,j]+tq*a[Q,j])
                row[i]=row[i]-(tp*row[P]+tq*row[Q])
            for n in range(p+1,8):
                vp,vq=V[n][P],V[n][Q]
                for i in range(Q+1,8):
                    tp,tq=t[i]
                    V[n][i]=V[n][i]-(tp*vp+tq*vq)
                E[n]=E[n]-(vp*yp+vq*yq)
            sp=lax.rsqrt(aa)
            ba=bb/aa
            sq=lax.rsqrt(cc-bb*ba)
            out[P]=sp*row[P]
            out[Q]=sq*(row[Q]-ba*row[P])
        x=out[0]
        for i in range(1,8): x=jnp.where(sub==i,out[i],x)
        X.append(x)
    return X

def eliminate(T):
    lane=lax.broadcasted_iota(jnp.int32,(8,128),1)
    sub=lax.broadcasted_iota(jnp.int32,(8,128),0)
    for k in range(4):
        r0=64*k; off=r0%128; g0=r0-off
        E=[]
        for p in range(8):
            v=T[r0+8*p:r0+8*p+8,g0:g0+128]
            inb=(lane>=off)&(lane<off+64)
            eye=(lane==(64-off)+8*p+sub).astype(F32)
            E.append(jnp.where(inb,v,eye))
        X=factor64(E,off)
        Xm=jnp.concatenate(X,0)
        Li=Xm[:,64-off:128-off]
        Lh,Ll=split(Li)
        Tr=T[r0:r0+64,:]
        if k<3:
            Z=dot3(T[r0+64:256,r0:r0+64],(Lh,Ll),NT)
        Xk=dot3((Lh,Ll),Tr)
        if k<3:
            T[r0+64:256,:]=T[r0+64:256,:]-dot3(Z,Xk)
        T[r0:r0+64,:]=Xk
        for p in range(8):
            rr=r0+8*p
            c=lax.broadcasted_iota(jnp.int32,(8,256),1); rw=lax.broadcasted_iota(jnp.int32,(8,256),0)+rr
            T[rr:rr+8,0:256]=jnp.where(c>=rw,T[rr:rr+8,0:256],0.0)
            T[rr:rr+8,512:768]=jnp.where(c<=rw,T[rr:rr+8,512:768],0.0)


def level_kernel(factor, s_ref, w_ref, p_ref, other_ref, otherp_ref, snew_ref, wnew_ref, q_ref, T):
    s, w = s_ref[...], w_ref[...]
    so, wo = other_ref[0:256, :], other_ref[256:512, :]
    if factor is not None:
        s = s - factor * dot3(p_ref[...], wo)
        so = so - factor * dot3(otherp_ref[...], w)
    mt = split(jnp.concatenate([s, so], axis=0).T)
    gram = dot3(mt, jnp.concatenate([s, so], axis=0))
    cross = dot3(mt, jnp.concatenate([w, wo], axis=0))
    rows = lax.broadcasted_iota(jnp.int32, (256, 256), 0)
    columns = lax.broadcasted_iota(jnp.int32, (256, 256), 1)
    eye = rows == columns
    trace = jnp.sum(jnp.where(eye, gram, 0.0))
    shift = 0.001 * (trace / 256.0 + 1e-6)
    T[:, 0:256] = gram + jnp.where(eye, shift, 0.0)
    T[:, 256:512] = cross
    T[:, 512:768] = jnp.where(eye, 1.0, 0.0)
    eliminate(T)
    snew_ref[...] = T[:, 0:256]
    wnew_ref[...] = T[:, 256:512]
    q_ref[...] = dot3(s, T[:, 512:768], NT)


def level_step(factor, s, w, p, other, other_p):
    square = jax.ShapeDtypeStruct((256, 256), F32)
    vmem = pl.BlockSpec(memory_space=pltpu.VMEM)
    return pl.pallas_call(
        lambda *refs: level_kernel(factor, *refs),
        out_shape=[square] * 3,
        in_specs=[vmem] * 5,
        out_specs=[vmem] * 3,
        scratch_shapes=[pltpu.VMEM((256, 768), F32)],
        compiler_params=pltpu.CompilerParams(vmem_limit_bytes=32 << 20),
        cost_estimate=pl.CostEstimate(flops=1 << 30, bytes_accessed=1 << 21, transcendentals=0),
    )(s, w, p, other, other_p)


def exchange(value, level):
    axis, bit, count = ("col", level, 8) if level < 3 else ("row", level - 3, 16)
    return lax.ppermute(value, axis, [(i, i ^ (1 << bit)) for i in range(count)])


def shards(front, tile_mask, probes, coupling):
    row_index = lax.axis_index("row")
    col_index = lax.axis_index("col")
    leaf_probe = lax.ppermute(
        probes, ("row", "col"), [((d % 16) * 8 + d // 16, d) for d in range(128)]
    )
    probe_block = lax.all_gather(probes, "row", axis=0, tiled=True)
    tile_above = row_index * 8 + jnp.arange(8, dtype=jnp.int32)
    tile_across = col_index * 16 + jnp.arange(16, dtype=jnp.int32)
    keep = tile_mask * (tile_above[:, None] // 2 != tile_across[None, :] // 2).astype(jnp.int32)
    masked = front.reshape(8, 256, 16, 256) * keep.astype(BF)[:, None, :, None]
    partial = jnp.dot(masked.reshape(front.shape), probe_block, preferred_element_type=F32)
    sample = lax.psum_scatter(partial, "col", scatter_dimension=0, tiled=True)
    others_p, p = [], coupling
    sums_p = [coupling]
    for level in range(7):
        others_p.append(exchange(sums_p[-1], level))
        sums_p.append(sums_p[-1] + others_p[-1])
    s, w = sample, leaf_probe.astype(F32)
    halves = []
    for level in range(7):
        other = exchange(jnp.concatenate([s, w], axis=0), level)
        factor = None if level == 0 else 2.0 ** (-level / 2.0)
        s, w, q = level_step(factor, s, w, sums_p[level], other, others_p[level])
        halves.append(q)
    return halves[0], jnp.stack(halves[1:], axis=0)


def solution(mesh):
    in_specs = (P("row", "col"), P("row", "col"), P(("col", "row"), None), P(("row", "col"), None))
    out_specs = (P(("row", "col"), None), P(None, ("row", "col"), None))
    return jax.shard_map(shards, mesh=mesh, in_specs=in_specs, out_specs=out_specs, check_vma=False)
```

```python
import jax
import jax.numpy as jnp
from jax import lax
from jax.experimental import pallas as pl
from jax.experimental.pallas import tpu as pltpu
from jax.sharding import PartitionSpec as P

MESH = pl.DeviceIdType.MESH
F32=jnp.float32; BF=jnp.bfloat16

def split(x):
    h=x.astype(BF); l=(x-h.astype(F32)).astype(BF); return h,l
def dg(a,b,dims):
    return lax.dot_general(a,b,(dims,((),())),preferred_element_type=F32)
NN=((1,),(0,)); NT=((1,),(1,)); TN=((0,),(0,))
def dot3(a,b,dims=NN):
    ah,al=a if isinstance(a,tuple) else split(a)
    bh,bl=b if isinstance(b,tuple) else split(b)
    return dg(ah,bh,dims)+(dg(ah,bl,dims)+dg(al,bh,dims))

def lanes(v,c): return jnp.broadcast_to(v[:,c:c+1],(8,128))
def subs(v,i): return jnp.broadcast_to(v[i:i+1,:],(8,128))

def factor64(E,off):
    sub=lax.broadcasted_iota(jnp.int32,(8,128),0)
    E=list(E); X=[]
    for p in range(8):
        row=[subs(E[p],i) for i in range(8)]
        a={}
        for i in range(8):
            for j in range(i,8):
                a[i,j]=lanes(row[i],off+8*p+j)
        V={}
        for n in range(p+1,8):
            V[n]=[lanes(E[n],off+8*p+k) for k in range(8)]
        out=[None]*8
        for m in range(4):
            P,Q=2*m,2*m+1
            aa,bb,cc=a[P,P],a[P,Q],a[Q,Q]
            det=aa*cc-bb*bb
            r=1.0/det
            ra=cc*r; rb=bb*r; rc=aa*r
            yp=ra*row[P]-rb*row[Q]
            yq=rc*row[Q]-rb*row[P]
            t={}
            for i in range(Q+1,8):
                u,v=a[P,i],a[Q,i]
                tp=(cc*u-bb*v)*r
                tq=(aa*v-bb*u)*r
                t[i]=(tp,tq)
                for j in range(i,8):
                    a[i,j]=a[i,j]-(tp*a[P,j]+tq*a[Q,j])
                row[i]=row[i]-(tp*row[P]+tq*row[Q])
            for n in range(p+1,8):
                vp,vq=V[n][P],V[n][Q]
                for i in range(Q+1,8):
                    tp,tq=t[i]
                    V[n][i]=V[n][i]-(tp*vp+tq*vq)
                E[n]=E[n]-(vp*yp+vq*yq)
            sp=lax.rsqrt(aa)
            ba=bb/aa
            sq=lax.rsqrt(cc-bb*ba)
            out[P]=sp*row[P]
            out[Q]=sq*(row[Q]-ba*row[P])
        x=out[0]
        for i in range(1,8): x=jnp.where(sub==i,out[i],x)
        X.append(x)
    return X


def eliminate(T, after_block):
    lane = lax.broadcasted_iota(jnp.int32, (8, 128), 1)
    sub = lax.broadcasted_iota(jnp.int32, (8, 128), 0)
    for k in range(4):
        r0 = 64 * k
        off = r0 % 128
        g0 = r0 - off
        E = []
        for p in range(8):
            v = T[r0 + 8 * p : r0 + 8 * p + 8, g0 : g0 + 128]
            inside = (lane >= off) & (lane < off + 64)
            eye = (lane == (64 - off) + 8 * p + sub).astype(F32)
            E.append(jnp.where(inside, v, eye))
        X = jnp.concatenate(factor64(E, off), 0)
        inv = split(X[:, 64 - off : 128 - off])
        block = T[r0 : r0 + 64, :]
        if k < 3:
            Z = dot3(T[r0 + 64 : 256, r0 : r0 + 64], inv, NT)
        Xk = dot3(inv, block)
        rows = lax.broadcasted_iota(jnp.int32, (64, 256), 0) + r0
        columns = lax.broadcasted_iota(jnp.int32, (64, 256), 1)
        T[r0 : r0 + 64, 0:256] = jnp.where(columns >= rows, Xk[:, 0:256], 0.0)
        T[r0 : r0 + 64, 256:512] = Xk[:, 256:512]
        T[r0 : r0 + 64, 512:768] = jnp.where(columns <= rows, Xk[:, 512:768], 0.0)
        after_block(k)
        if k < 3:
            T[r0 + 64 : 256, :] = T[r0 + 64 : 256, :] - dot3(Z, Xk)


def by_level(level, values):
    out = values[-1]
    for i in range(len(values) - 2, -1, -1):
        out = jnp.where(level == i, values[i], out)
    return out


def tree_kernel(s_ref, w_ref, p_ref, leaf_ref, upper_ref, T, recv, p_own, p_oth,
                send_sem, recv_sem, corner_sem, p_send, p_recv):
    me = lax.axis_index("row") * 8 + lax.axis_index("col")

    def partner(level):
        if isinstance(level, int):
            h = 2**level
        else:
            h = by_level(level, [1, 2, 4, 8, 16, 32, 64])
        other = me + h * (1 - 2 * ((me // h) % 2))
        return (other // 8, other % 8)

    def state_copy(level, k):
        c0 = 0 if k < 2 else 128
        return pltpu.make_async_remote_copy(
            src_ref=T.at[64 * k : 64 * k + 64, c0:512],
            dst_ref=recv.at[level, 64 * k : 64 * k + 64, c0:512],
            send_sem=send_sem.at[k],
            recv_sem=recv_sem.at[level, k],
            device_id=partner(level),
            device_id_type=MESH,
        )

    def p_copy(level):
        return pltpu.make_async_remote_copy(
            src_ref=p_own.at[level],
            dst_ref=p_oth.at[level],
            send_sem=p_send.at[level],
            recv_sem=p_recv.at[level],
            device_id=partner(level),
            device_id_type=MESH,
        )

    barrier = pltpu.get_barrier_semaphore()
    for level in range(7):
        pl.semaphore_signal(barrier, inc=1, device_id=partner(level), device_id_type=MESH)
    T[:, 0:256] = s_ref[...]
    T[:, 256:512] = w_ref[...].astype(F32)
    p_own[0] = p_ref[...]
    for level in range(1, 7):
        recv[level, 128:256, 0:128] = jnp.zeros((128, 128), F32)
    pl.semaphore_wait(barrier, 7)
    corner = pltpu.make_async_remote_copy(
        src_ref=T.at[128:256, 0:128],
        dst_ref=recv.at[0, 128:256, 0:128],
        send_sem=corner_sem.at[0],
        recv_sem=corner_sem.at[1],
        device_id=partner(0),
        device_id_type=MESH,
    )
    for k in range(4):
        state_copy(0, k).start()
    corner.start()
    p_copy(0).start()
    corner.wait()
    p_copy(0).wait()
    p_own[1] = p_own[0] + p_oth[0]
    p_copy(1).start()

    rows = lax.broadcasted_iota(jnp.int32, (256, 256), 0)
    columns = lax.broadcasted_iota(jnp.int32, (256, 256), 1)
    eye = rows == columns

    def level_body(level, carry):
        factor = by_level(level, [0.0] + [2.0 ** (-l / 2.0) for l in range(1, 7)])
        for k in range(4):
            state_copy(level, k).wait()
        s, w = T[:, 0:256], T[:, 256:512]
        so, wo = recv[level, :, 0:256], recv[level, :, 256:512]
        s = s - factor * dot3(p_own[level], wo)
        so = so - factor * dot3(p_oth[level], w)
        M = jnp.concatenate([s, so], axis=0)
        mt = split(M.T)
        gram = dot3(mt, M)
        cross = dot3(mt, jnp.concatenate([w, wo], axis=0))
        trace = jnp.sum(jnp.where(eye, gram, 0.0))
        shift = 0.001 * (trace / 256.0 + 1e-6)
        T[:, 0:256] = gram + jnp.where(eye, shift, 0.0)
        T[:, 256:512] = cross
        T[:, 512:768] = jnp.where(eye, 1.0, 0.0)

        def after_block(k):
            @pl.when(level < 6)
            def _():
                state_copy(level + 1, k).start()

            if k == 1:

                @pl.when(level < 6)
                def _():
                    p_copy(level + 1).wait()

                @pl.when(level < 5)
                def _():
                    p_own[level + 2] = p_own[level + 1] + p_oth[level + 1]
                    p_copy(level + 2).start()

        eliminate(T, after_block)
        q = dot3(s, T[:, 512:768], NT)

        @pl.when(level == 0)
        def _():
            leaf_ref[...] = q

        @pl.when(level > 0)
        def _():
            upper_ref[level - 1] = q

        return carry

    lax.fori_loop(0, 7, level_body, 0)


def tree(sample, leaf_probe, coupling):
    vmem = pl.BlockSpec(memory_space=pltpu.VMEM)
    return pl.pallas_call(
        tree_kernel,
        out_shape=[
            jax.ShapeDtypeStruct((256, 256), F32),
            jax.ShapeDtypeStruct((6, 256, 256), F32),
        ],
        in_specs=[vmem] * 3,
        out_specs=[vmem] * 2,
        scratch_shapes=[
            pltpu.VMEM((256, 768), F32),
            pltpu.VMEM((7, 256, 512), F32),
            pltpu.VMEM((7, 256, 256), F32),
            pltpu.VMEM((7, 256, 256), F32),
            pltpu.SemaphoreType.DMA((4,)),
            pltpu.SemaphoreType.DMA((7, 4)),
            pltpu.SemaphoreType.DMA((2,)),
            pltpu.SemaphoreType.DMA((7,)),
            pltpu.SemaphoreType.DMA((7,)),
        ],
        compiler_params=pltpu.CompilerParams(
            collective_id=1, has_side_effects=True, vmem_limit_bytes=40 << 20
        ),
        cost_estimate=pl.CostEstimate(flops=7 << 30, bytes_accessed=7 << 21, transcendentals=0),
    )(sample, leaf_probe, coupling)


def shards(front, tile_mask, probes, coupling):
    row_index = lax.axis_index("row")
    col_index = lax.axis_index("col")
    leaf_probe = lax.ppermute(
        probes, ("row", "col"), [((d % 16) * 8 + d // 16, d) for d in range(128)]
    )
    probe_block = lax.all_gather(probes, "row", axis=0, tiled=True)
    tile_above = row_index * 8 + jnp.arange(8, dtype=jnp.int32)
    tile_across = col_index * 16 + jnp.arange(16, dtype=jnp.int32)
    keep = tile_mask * (tile_above[:, None] // 2 != tile_across[None, :] // 2).astype(jnp.int32)
    masked = front.reshape(8, 256, 16, 256) * keep.astype(BF)[:, None, :, None]
    partial = jnp.dot(masked.reshape(front.shape), probe_block, preferred_element_type=F32)
    sample = lax.psum_scatter(partial, "col", scatter_dimension=0, tiled=True)
    leaf, upper = tree(sample, leaf_probe, coupling)
    return leaf, upper


def solution(mesh):
    in_specs = (P("row", "col"), P("row", "col"), P(("col", "row"), None), P(("row", "col"), None))
    out_specs = (P(("row", "col"), None), P(None, ("row", "col"), None))
    return jax.shard_map(shards, mesh=mesh, in_specs=in_specs, out_specs=out_specs, check_vma=False)
```

```python
import jax
import jax.numpy as jnp
from jax import lax
from jax.experimental import pallas as pl
from jax.experimental.pallas import tpu as pltpu
from jax.sharding import PartitionSpec as P

MESH = pl.DeviceIdType.MESH
F32=jnp.float32; BF=jnp.bfloat16

def split(x):
    h=x.astype(BF); l=(x-h.astype(F32)).astype(BF); return h,l
def dg(a,b,dims):
    return lax.dot_general(a,b,(dims,((),())),preferred_element_type=F32)
NN=((1,),(0,)); NT=((1,),(1,)); TN=((0,),(0,))
def dot3(a,b,dims=NN):
    ah,al=a if isinstance(a,tuple) else split(a)
    bh,bl=b if isinstance(b,tuple) else split(b)
    return dg(ah,bh,dims)+(dg(ah,bl,dims)+dg(al,bh,dims))

def lanes(v,c): return jnp.broadcast_to(v[:,c:c+1],(8,128))
def subs(v,i): return jnp.broadcast_to(v[i:i+1,:],(8,128))

def factor64(E,off):
    sub=lax.broadcasted_iota(jnp.int32,(8,128),0)
    E=list(E); X=[]
    for p in range(8):
        row=[subs(E[p],i) for i in range(8)]
        a={}
        for i in range(8):
            for j in range(i,8):
                a[i,j]=lanes(row[i],off+8*p+j)
        V={}
        for n in range(p+1,8):
            V[n]=[lanes(E[n],off+8*p+k) for k in range(8)]
        out=[None]*8
        for m in range(4):
            P,Q=2*m,2*m+1
            aa,bb,cc=a[P,P],a[P,Q],a[Q,Q]
            det=aa*cc-bb*bb
            r=1.0/det
            ra=cc*r; rb=bb*r; rc=aa*r
            yp=ra*row[P]-rb*row[Q]
            yq=rc*row[Q]-rb*row[P]
            t={}
            for i in range(Q+1,8):
                u,v=a[P,i],a[Q,i]
                tp=(cc*u-bb*v)*r
                tq=(aa*v-bb*u)*r
                t[i]=(tp,tq)
                for j in range(i,8):
                    a[i,j]=a[i,j]-(tp*a[P,j]+tq*a[Q,j])
                row[i]=row[i]-(tp*row[P]+tq*row[Q])
            for n in range(p+1,8):
                vp,vq=V[n][P],V[n][Q]
                for i in range(Q+1,8):
                    tp,tq=t[i]
                    V[n][i]=V[n][i]-(tp*vp+tq*vq)
                E[n]=E[n]-(vp*yp+vq*yq)
            sp=lax.rsqrt(aa)
            ba=bb/aa
            sq=lax.rsqrt(cc-bb*ba)
            out[P]=sp*row[P]
            out[Q]=sq*(row[Q]-ba*row[P])
        x=out[0]
        for i in range(1,8): x=jnp.where(sub==i,out[i],x)
        X.append(x)
    return X


def eliminate(T, after_block):
    lane = lax.broadcasted_iota(jnp.int32, (8, 128), 1)
    sub = lax.broadcasted_iota(jnp.int32, (8, 128), 0)
    for k in range(4):
        r0 = 64 * k
        off = r0 % 128
        g0 = r0 - off
        E = []
        for p in range(8):
            v = T[r0 + 8 * p : r0 + 8 * p + 8, g0 : g0 + 128]
            inside = (lane >= off) & (lane < off + 64)
            eye = (lane == (64 - off) + 8 * p + sub).astype(F32)
            E.append(jnp.where(inside, v, eye))
        X = jnp.concatenate(factor64(E, off), 0)
        inv = split(X[:, 64 - off : 128 - off])
        block = T[r0 : r0 + 64, :]
        if k < 3:
            Z = dot3(T[r0 + 64 : 256, r0 : r0 + 64], inv, NT)
        Xk = dot3(inv, block)
        rows = lax.broadcasted_iota(jnp.int32, (64, 256), 0) + r0
        columns = lax.broadcasted_iota(jnp.int32, (64, 256), 1)
        T[r0 : r0 + 64, 0:256] = jnp.where(columns >= rows, Xk[:, 0:256], 0.0)
        T[r0 : r0 + 64, 256:512] = Xk[:, 256:512]
        T[r0 : r0 + 64, 512:768] = jnp.where(columns <= rows, Xk[:, 512:768], 0.0)
        after_block(k)
        if k < 3:
            T[r0 + 64 : 256, :] = T[r0 + 64 : 256, :] - dot3(Z, Xk)


def by_level(level, values):
    out = values[-1]
    for i in range(len(values) - 2, -1, -1):
        out = jnp.where(level == i, values[i], out)
    return out


def tree_kernel(s_ref, w_ref, p_ref, leaf_ref, upper_ref, T, recv, p_own, p_oth,
                send_sem, recv_sem, corner_sem, p_send, p_recv):
    me = lax.axis_index("row") * 8 + lax.axis_index("col")

    def partner(level):
        if isinstance(level, int):
            h = 2**level
        else:
            h = by_level(level, [1, 2, 4, 8, 16, 32, 64])
        other = me + h * (1 - 2 * ((me // h) % 2))
        return (other // 8, other % 8)

    def state_copy(level, k):
        c0 = 0 if k < 2 else 128
        return pltpu.make_async_remote_copy(
            src_ref=T.at[64 * k : 64 * k + 64, c0:512],
            dst_ref=recv.at[level, 64 * k : 64 * k + 64, c0:512],
            send_sem=send_sem.at[k],
            recv_sem=recv_sem.at[level, k],
            device_id=partner(level),
            device_id_type=MESH,
        )

    def p_copy(level):
        return pltpu.make_async_remote_copy(
            src_ref=p_own.at[level],
            dst_ref=p_oth.at[level],
            send_sem=p_send.at[level],
            recv_sem=p_recv.at[level],
            device_id=partner(level),
            device_id_type=MESH,
        )

    barrier = pltpu.get_barrier_semaphore()
    for level in range(7):
        pl.semaphore_signal(barrier, inc=1, device_id=partner(level), device_id_type=MESH)
    T[:, 0:256] = s_ref[...]
    T[:, 256:512] = w_ref[...].astype(F32)
    p_own[0] = p_ref[...]
    for level in range(1, 7):
        recv[level, 128:256, 0:128] = jnp.zeros((128, 128), F32)
    pl.semaphore_wait(barrier, 7)
    corner = pltpu.make_async_remote_copy(
        src_ref=T.at[128:256, 0:128],
        dst_ref=recv.at[0, 128:256, 0:128],
        send_sem=corner_sem.at[0],
        recv_sem=corner_sem.at[1],
        device_id=partner(0),
        device_id_type=MESH,
    )
    for k in range(4):
        state_copy(0, k).start()
    corner.start()
    p_copy(0).start()
    corner.wait()
    p_copy(0).wait()
    p_own[1] = p_own[0] + p_oth[0]
    p_copy(1).start()

    rows = lax.broadcasted_iota(jnp.int32, (256, 256), 0)
    columns = lax.broadcasted_iota(jnp.int32, (256, 256), 1)
    eye = rows == columns

    def level_body(level, carry):
        factor = by_level(level, [0.0] + [2.0 ** (-l / 2.0) for l in range(1, 7)])
        for k in range(4):
            state_copy(level, k).wait()
        s, w = T[:, 0:256], T[:, 256:512]
        so, wo = recv[level, :, 0:256], recv[level, :, 256:512]
        s = s - factor * dot3(p_own[level], wo)
        so = so - factor * dot3(p_oth[level], w)
        M = jnp.concatenate([s, so], axis=0)
        mt = split(M.T)
        gram = dot3(mt, M)
        cross = dot3(mt, jnp.concatenate([w, wo], axis=0))
        trace = jnp.sum(jnp.where(eye, gram, 0.0))
        shift = 0.001 * (trace / 256.0 + 1e-6)
        T[:, 0:256] = gram + jnp.where(eye, shift, 0.0)
        T[:, 256:512] = cross
        T[:, 512:768] = jnp.where(eye, 1.0, 0.0)

        def after_block(k):
            @pl.when(level < 6)
            def _():
                state_copy(level + 1, k).start()

            if k == 1:

                @pl.when(level < 6)
                def _():
                    p_copy(level + 1).wait()

                @pl.when(level < 5)
                def _():
                    p_own[level + 2] = p_own[level + 1] + p_oth[level + 1]
                    p_copy(level + 2).start()

        eliminate(T, after_block)
        q = dot3(s, T[:, 512:768], NT)

        @pl.when(level == 0)
        def _():
            leaf_ref[...] = q

        @pl.when(level > 0)
        def _():
            upper_ref[level - 1] = q

        return carry

    lax.fori_loop(0, 7, level_body, 0)


def tree(sample, leaf_probe, coupling):
    vmem = pl.BlockSpec(memory_space=pltpu.VMEM)
    return pl.pallas_call(
        tree_kernel,
        out_shape=[
            jax.ShapeDtypeStruct((256, 256), F32),
            jax.ShapeDtypeStruct((6, 256, 256), F32),
        ],
        in_specs=[vmem] * 3,
        out_specs=[vmem] * 2,
        scratch_shapes=[
            pltpu.VMEM((256, 768), F32),
            pltpu.VMEM((7, 256, 512), F32),
            pltpu.VMEM((7, 256, 256), F32),
            pltpu.VMEM((7, 256, 256), F32),
            pltpu.SemaphoreType.DMA((4,)),
            pltpu.SemaphoreType.DMA((7, 4)),
            pltpu.SemaphoreType.DMA((2,)),
            pltpu.SemaphoreType.DMA((7,)),
            pltpu.SemaphoreType.DMA((7,)),
        ],
        compiler_params=pltpu.CompilerParams(
            collective_id=1, has_side_effects=True, vmem_limit_bytes=40 << 20
        ),
        cost_estimate=pl.CostEstimate(flops=7 << 30, bytes_accessed=7 << 21, transcendentals=0),
    )(sample, leaf_probe, coupling)


def front_kernel(front_ref, keep_ref, probes_ref, s_ref, w_ref, F, B, acc, from_core, from_x, leaf,
                 f_sem, near_send, near_recv, far_send, far_recv, c_send, c_recv, x_send, x_recv, l_sem):
    row, col = lax.axis_index("row"), lax.axis_index("col")
    z, y = row // 4, row % 4
    x, c = col // 2, col % 2
    me = row * 8 + col
    target = col * 16 + row
    source = (me % 16, me // 16)
    moved = target != me

    def at(dz, dy):
        return ((z + dz + 4) % 4 * 4 + (y + dy + 4) % 4, col)

    def along_x(d, other):
        core = 1 - c if other else c
        return (row, (x + d) % 4 * 2 + core)

    def half_rows(dz, dy, h):
        block = (z + dz + 4) % 4 * 4 + (y + dy + 4) % 4
        return pl.ds(pl.multiple_of(block * 256 + h * 128, 128), 128)

    def columns_of(d):
        return pl.ds(pl.multiple_of((z + 4 - d) % 4 * 1024, 1024), 1024)

    def remote(src, dst, send, recv, device):
        return pltpu.make_async_remote_copy(
            src_ref=src, dst_ref=dst, send_sem=send, recv_sem=recv, device_id=device, device_id_type=MESH
        )

    def load(d):
        return pltpu.make_async_copy(front_ref.at[:, columns_of(d)], F.at[:, columns_of(d)], f_sem.at[d])

    def near(h, d):
        r = half_rows(0, 0, h)
        return remote(B.at[r], B.at[r], near_send.at[h, d - 1], near_recv.at[h, d - 1],
                      at(0, d) if h == 0 else at(d, 0))

    def far(h, held, d):
        r = half_rows(0, -held, 0) if h == 0 else half_rows(-held, 0, 1)
        return remote(B.at[r], B.at[r], far_send.at[h, held, d - 1], far_recv.at[h, held, d - 1],
                      at(d, 0) if h == 0 else at(0, d))

    def to_core(d):
        t = pl.ds(pl.multiple_of(((x + d) % 4 * 2 + 1 - c) * 256, 256), 256)
        return remote(acc.at[t], from_core.at[d], c_send.at[d], c_recv.at[d], along_x(0, True))

    def to_x(d):
        t = pl.ds(pl.multiple_of(((x + d) % 4 * 2 + c) * 256, 256), 256)
        return remote(acc.at[t], from_x.at[d - 1], x_send.at[d - 1], x_recv.at[d - 1], along_x(d, False))

    def to_leaf():
        return remote(probes_ref, leaf, l_sem.at[0], l_sem.at[1], (target // 8, target % 8))

    order = (0, 1, 3, 2)
    for d in order:
        load(d).start()
    barrier = pltpu.get_barrier_semaphore()
    peers = [at(d, 0) for d in (1, 2, 3)] + [at(0, d) for d in (1, 2, 3)]
    peers += [along_x(d, False) for d in (1, 2, 3)] + [along_x(0, True)]
    for peer in peers:
        pl.semaphore_signal(barrier, inc=1, device_id=peer, device_id_type=MESH)
    pl.semaphore_signal(barrier, inc=1, device_id=source, device_id_type=MESH)

    own = pl.ds(pl.multiple_of(row * 256, 256), 256)
    B[own, :] = probes_ref[...]
    pl.semaphore_wait(barrier, 11)

    for d in (1, 3, 2):
        near(0, d).start()
        near(1, d).start()
    for d in (1, 3, 2):
        far(0, 0, d).start()
        far(1, 0, d).start()
    for held in (1, 3, 2):
        near(0, held).wait_recv()
        near(1, held).wait_recv()
        for d in (1, 3, 2):
            far(0, held, d).start()
            far(1, held, d).start()

    @pl.when(moved)
    def _():
        to_leaf().start()

    @pl.when(jnp.logical_not(moved))
    def _():
        leaf[...] = probes_ref[...]

    def product(a, d):
        r = pl.ds(pl.multiple_of(a * 256, 256), 256)
        k = keep_ref[pl.ds(a, 1), columns_of(d)].astype(BF)
        return jnp.dot(F[r, columns_of(d)] * k, B[columns_of(d), :], preferred_element_type=F32)

    for d in order:
        load(d).wait()
        if d == 0:
            for e in (1, 2, 3):
                far(1, 0, e).wait_recv()
        else:
            for e in range(4):
                far(0, e, d).wait_recv()
            for e in (1, 2, 3):
                far(1, d, e).wait_recv()
        if d != order[-1]:

            def body(a, carry):
                r = pl.ds(pl.multiple_of(a * 256, 256), 256)
                p = product(a, d)
                acc[r, :] = p if d == 0 else acc[r, :] + p
                return carry

            lax.fori_loop(0, 8, body, 0)

    def finish(e):
        to_core(e).wait_recv()
        r = pl.ds(pl.multiple_of(((x + e) % 4 * 2 + c) * 256, 256), 256)
        acc[r, :] = acc[r, :] + from_core[e]
        if e:
            to_x(e).start()

    ahead = None
    for e in (2, 1, 3, 0):
        for other in (True, False):
            a = (x + e) % 4 * 2 + (1 - c if other else c)
            r = pl.ds(pl.multiple_of(a * 256, 256), 256)
            acc[r, :] = acc[r, :] + product(a, order[-1])
            if other:
                to_core(e).start()
        if ahead is not None:
            finish(ahead)
        ahead = e
    finish(0)
    total = acc[pl.ds(pl.multiple_of(col * 256, 256), 256), :]
    for d in (1, 3, 2):
        to_x(d).wait_recv()
        total = total + from_x[d - 1]
    s_ref[...] = total

    @pl.when(moved)
    def _():
        to_leaf().wait()

    w_ref[...] = leaf[...]
    for h in (0, 1):
        for d in (1, 2, 3):
            near(h, d).wait_send()
            for held in range(4):
                far(h, held, d).wait_send()
    for d in range(4):
        to_core(d).wait_send()
    for d in (1, 2, 3):
        to_x(d).wait_send()


def samples(front, keep, probes):
    vmem = pl.BlockSpec(memory_space=pltpu.VMEM)
    return pl.pallas_call(
        front_kernel,
        out_shape=[jax.ShapeDtypeStruct((256, 256), F32), jax.ShapeDtypeStruct((256, 256), BF)],
        in_specs=[pl.BlockSpec(memory_space=pl.ANY), vmem, vmem],
        out_specs=[vmem] * 2,
        scratch_shapes=[
            pltpu.VMEM((2048, 4096), BF),
            pltpu.VMEM((4096, 256), BF),
            pltpu.VMEM((2048, 256), F32),
            pltpu.VMEM((4, 256, 256), F32),
            pltpu.VMEM((3, 256, 256), F32),
            pltpu.VMEM((256, 256), BF),
            pltpu.SemaphoreType.DMA((4,)),
            pltpu.SemaphoreType.DMA((2, 3)),
            pltpu.SemaphoreType.DMA((2, 3)),
            pltpu.SemaphoreType.DMA((2, 4, 3)),
            pltpu.SemaphoreType.DMA((2, 4, 3)),
            pltpu.SemaphoreType.DMA((4,)),
            pltpu.SemaphoreType.DMA((4,)),
            pltpu.SemaphoreType.DMA((3,)),
            pltpu.SemaphoreType.DMA((3,)),
            pltpu.SemaphoreType.DMA((2,)),
        ],
        compiler_params=pltpu.CompilerParams(
            collective_id=2, has_side_effects=True, vmem_limit_bytes=44 << 20
        ),
        cost_estimate=pl.CostEstimate(flops=1 << 32, bytes_accessed=1 << 24, transcendentals=0),
    )(front, keep, probes)


def shards(front, tile_mask, probes, coupling):
    row_index = lax.axis_index("row")
    col_index = lax.axis_index("col")
    tile_above = row_index * 8 + jnp.arange(8, dtype=jnp.int32)
    tile_across = col_index * 16 + jnp.arange(16, dtype=jnp.int32)
    keep = tile_mask * (tile_above[:, None] // 2 != tile_across[None, :] // 2).astype(jnp.int32)
    keep = jnp.repeat(keep.astype(F32), 256, axis=1)
    sample, leaf_probe = samples(front, keep, probes)
    leaf, upper = tree(sample, leaf_probe, coupling)
    return leaf, upper


def solution(mesh):
    in_specs = (P("row", "col"), P("row", "col"), P(("col", "row"), None), P(("row", "col"), None))
    out_specs = (P(("row", "col"), None), P(None, ("row", "col"), None))
    return jax.shard_map(shards, mesh=mesh, in_specs=in_specs, out_specs=out_specs, check_vma=False)
```

```python
import jax
import jax.numpy as jnp
from jax import lax
from jax.experimental import pallas as pl
from jax.experimental.pallas import tpu as pltpu
from jax.sharding import PartitionSpec as P

MESH = pl.DeviceIdType.MESH
F32=jnp.float32; BF=jnp.bfloat16

def split(x):
    h=x.astype(BF); l=(x-h.astype(F32)).astype(BF); return h,l
def dg(a,b,dims):
    return lax.dot_general(a,b,(dims,((),())),preferred_element_type=F32)
NN=((1,),(0,)); NT=((1,),(1,)); TN=((0,),(0,))
def dot3(a,b,dims=NN):
    ah,al=a if isinstance(a,tuple) else split(a)
    bh,bl=b if isinstance(b,tuple) else split(b)
    return dg(ah,bh,dims)+(dg(ah,bl,dims)+dg(al,bh,dims))

def lanes(v,c): return jnp.broadcast_to(v[:,c:c+1],(8,128))
def subs(v,i): return jnp.broadcast_to(v[i:i+1,:],(8,128))

def rcp(x):
    return pltpu.reciprocal(x,approx=True)
def factor64(E,off):
    sub=lax.broadcasted_iota(jnp.int32,(8,128),0)
    E=list(E); X=[]
    D=[lanes(E[0],off+j) for j in range(8)]
    for p in range(8):
        V={n:[lanes(E[n],off+8*p+k) for k in range(8)] for n in range(p+1,8)}
        ahead=[lanes(E[p+1],off+8*p+8+j) for j in range(8)] if p<7 else None
        out=None
        for m in range(4):
            P,Q=2*m,2*m+1
            vp,vq=D[P],D[Q]
            aa,bb,cc=subs(vp,P),subs(vq,P),subs(vq,Q)
            r=rcp(aa*cc-bb*bb)
            ep,eq=subs(E[p],P),subs(E[p],Q)
            yp=(cc*ep-bb*eq)*r
            yq=(aa*eq-bb*ep)*r
            zp=(cc*vp-bb*vq)*r
            zq=(aa*vq-bb*vp)*r
            z={j:(subs(zp,j),subs(zq,j)) for j in range(Q+1,8)}
            if m<3:
                mp=jnp.where(sub>Q,vp,0.0); mq=jnp.where(sub>Q,vq,0.0)
                for j in range(Q+1,8):
                    D[j]=D[j]-(mp*z[j][0]+mq*z[j][1])
                E[p]=E[p]-(mp*yp+mq*yq)
            for n in range(p+1,8):
                wp,wq=V[n][P],V[n][Q]
                if n==p+1:
                    tp=(cc*wp-bb*wq)*r
                    tq=(aa*wq-bb*wp)*r
                    for j in range(8):
                        ahead[j]=ahead[j]-(wp*subs(tp,j)+wq*subs(tq,j))
                for j in range(Q+1,8):
                    V[n][j]=V[n][j]-(wp*z[j][0]+wq*z[j][1])
                E[n]=E[n]-(wp*yp+wq*yq)
            ba=bb*rcp(aa)
            sp=lax.rsqrt(aa); sq=lax.rsqrt(cc-bb*ba)
            xp=sp*ep; xq=sq*(eq-ba*ep)
            out=xp if out is None else jnp.where(sub==P,xp,out)
            out=jnp.where(sub==Q,xq,out)
        X.append(out)
        D=ahead
    return X

def eliminate(T, after_block):
    lane = lax.broadcasted_iota(jnp.int32, (8, 128), 1)
    sub = lax.broadcasted_iota(jnp.int32, (8, 128), 0)
    for k in range(4):
        r0 = 64 * k
        off = r0 % 128
        g0 = r0 - off
        E = []
        for p in range(8):
            v = T[r0 + 8 * p : r0 + 8 * p + 8, g0 : g0 + 128]
            inside = (lane >= off) & (lane < off + 64)
            eye = (lane == (64 - off) + 8 * p + sub).astype(F32)
            E.append(jnp.where(inside, v, eye))
        X = jnp.concatenate(factor64(E, off), 0)
        inv = split(X[:, 64 - off : 128 - off])
        block = T[r0 : r0 + 64, :]
        if k < 3:
            Z = dot3(T[r0 + 64 : 256, r0 : r0 + 64], inv, NT)
        Xk = dot3(inv, block)
        rows = lax.broadcasted_iota(jnp.int32, (64, 256), 0) + r0
        columns = lax.broadcasted_iota(jnp.int32, (64, 256), 1)
        T[r0 : r0 + 64, 0:256] = jnp.where(columns >= rows, Xk[:, 0:256], 0.0)
        T[r0 : r0 + 64, 256:512] = Xk[:, 256:512]
        T[r0 : r0 + 64, 512:768] = jnp.where(columns <= rows, Xk[:, 512:768], 0.0)
        after_block(k)
        if k < 3:
            T[r0 + 64 : 256, :] = T[r0 + 64 : 256, :] - dot3(Z, Xk)


def by_level(level, values):
    out = values[-1]
    for i in range(len(values) - 2, -1, -1):
        out = jnp.where(level == i, values[i], out)
    return out


def whole_kernel(front_ref, keep_ref, probes_ref, p_ref, leaf_ref, upper_ref,
                 F, B, acc, from_core, from_x, leaf, T, recv, p_own, p_oth,
                 f_sem, near_send, near_recv, far_send, far_recv, c_send, c_recv, x_send, x_recv, l_sem,
                 d_send, d_recv, w_send, w_recv, p_send, p_recv):
    row, col = lax.axis_index("row"), lax.axis_index("col")
    z, y = row // 4, row % 4
    x, c = col // 2, col % 2
    me = row * 8 + col
    target = col * 16 + row
    source = (me % 16, me // 16)
    moved = target != me

    def at(dz, dy):
        return ((z + dz + 4) % 4 * 4 + (y + dy + 4) % 4, col)

    def along_x(d, other):
        core = 1 - c if other else c
        return (row, (x + d) % 4 * 2 + core)

    def half_rows(dz, dy, h):
        block = (z + dz + 4) % 4 * 4 + (y + dy + 4) % 4
        return pl.ds(pl.multiple_of(block * 256 + h * 128, 128), 128)

    def columns_of(d):
        return pl.ds(pl.multiple_of((z + 4 - d) % 4 * 1024, 1024), 1024)

    def remote(src, dst, send, recv, device):
        return pltpu.make_async_remote_copy(
            src_ref=src, dst_ref=dst, send_sem=send, recv_sem=recv, device_id=device, device_id_type=MESH
        )

    def load(d):
        return pltpu.make_async_copy(front_ref.at[:, columns_of(d)], F.at[:, columns_of(d)], f_sem.at[d])

    def near(h, d):
        r = half_rows(0, 0, h)
        return remote(B.at[r], B.at[r], near_send.at[h, d - 1], near_recv.at[h, d - 1],
                      at(0, d) if h == 0 else at(d, 0))

    def far(h, held, d):
        r = half_rows(0, -held, 0) if h == 0 else half_rows(-held, 0, 1)
        return remote(B.at[r], B.at[r], far_send.at[h, held, d - 1], far_recv.at[h, held, d - 1],
                      at(d, 0) if h == 0 else at(0, d))

    def to_core(d):
        t = pl.ds(pl.multiple_of(((x + d) % 4 * 2 + 1 - c) * 256, 256), 256)
        return remote(acc.at[t], from_core.at[d], c_send.at[d], c_recv.at[d], along_x(0, True))

    def to_x(d):
        t = pl.ds(pl.multiple_of(((x + d) % 4 * 2 + c) * 256, 256), 256)
        return remote(acc.at[t], from_x.at[d - 1], x_send.at[d - 1], x_recv.at[d - 1], along_x(d, False))

    def to_leaf():
        return remote(probes_ref, leaf, l_sem.at[0], l_sem.at[1], (target // 8, target % 8))

    def partner(level):
        h = 2**level if isinstance(level, int) else by_level(level, [1, 2, 4, 8, 16, 32, 64])
        other = me + h * (1 - 2 * ((me // h) % 2))
        return (other // 8, other % 8)

    def p_copy(level):
        return remote(p_own.at[level], p_oth.at[level], p_send.at[level], p_recv.at[level], partner(level))

    def p_step(level):
        p_copy(level).wait()
        p_own[level + 1] = p_own[level] + p_oth[level]

    def part(k, core):
        if k == 3:
            return pl.ds(192, 64), pl.ds(128, 384)
        c0 = 0 if k < 2 else 128
        return pl.ds(pl.multiple_of(64 * k + 32 * core, 32), 32), pl.ds(c0, 512 - c0)

    def direct(level, k):
        r, l = part(k, c)
        return remote(T.at[r, l], recv.at[level, r, l], d_send.at[k], d_recv.at[level, k], partner(level))

    def passed(level, k):
        r, l = part(k, c)
        return remote(recv.at[level, r, l], recv.at[level, r, l], w_send.at[k], w_recv.at[level, k], partner(0))

    order = (0, 1, 3, 2)
    for d in order:
        load(d).start()
    barrier = pltpu.get_barrier_semaphore()
    peers = [at(d, 0) for d in (1, 2, 3)] + [at(0, d) for d in (1, 2, 3)]
    peers += [along_x(d, False) for d in (1, 2, 3)] + [along_x(0, True)]
    for peer in peers:
        pl.semaphore_signal(barrier, inc=1, device_id=peer, device_id_type=MESH)
    pl.semaphore_signal(barrier, inc=1, device_id=source, device_id_type=MESH)

    own = pl.ds(pl.multiple_of(row * 256, 256), 256)
    B[own, :] = probes_ref[...]
    p_own[0] = p_ref[...]
    pl.semaphore_wait(barrier, 11)

    for d in (1, 3, 2):
        near(0, d).start()
        near(1, d).start()
    for d in (1, 3, 2):
        far(0, 0, d).start()
        far(1, 0, d).start()
    p_copy(0).start()
    for held in (1, 3, 2):
        near(0, held).wait_recv()
        near(1, held).wait_recv()
        for d in (1, 3, 2):
            far(0, held, d).start()
            far(1, held, d).start()

    @pl.when(moved)
    def _():
        to_leaf().start()

    @pl.when(jnp.logical_not(moved))
    def _():
        leaf[...] = probes_ref[...]

    p_step(0)
    p_copy(1).start()

    def product(a, d):
        r = pl.ds(pl.multiple_of(a * 256, 256), 256)
        k = keep_ref[pl.ds(a, 1), columns_of(d)].astype(BF)
        return jnp.dot(F[r, columns_of(d)] * k, B[columns_of(d), :], preferred_element_type=F32)

    for d in order:
        load(d).wait()
        if d == 0:
            for e in (1, 2, 3):
                far(1, 0, e).wait_recv()
        else:
            for e in range(4):
                far(0, e, d).wait_recv()
            for e in (1, 2, 3):
                far(1, d, e).wait_recv()
        if d != order[-1]:

            def body(a, carry):
                r = pl.ds(pl.multiple_of(a * 256, 256), 256)
                p = product(a, d)
                acc[r, :] = p if d == 0 else acc[r, :] + p
                return carry

            lax.fori_loop(0, 8, body, 0)
            if d == order[1]:
                p_step(1)
                p_copy(2).start()

    def finish(e):
        to_core(e).wait_recv()
        r = pl.ds(pl.multiple_of(((x + e) % 4 * 2 + c) * 256, 256), 256)
        acc[r, :] = acc[r, :] + from_core[e]
        if e:
            to_x(e).start()

    ahead = None
    for e in (2, 1, 3, 0):
        for other in (True, False):
            a = (x + e) % 4 * 2 + (1 - c if other else c)
            r = pl.ds(pl.multiple_of(a * 256, 256), 256)
            acc[r, :] = acc[r, :] + product(a, order[-1])
            if other:
                to_core(e).start()
        if ahead is not None:
            finish(ahead)
        ahead = e
    finish(0)
    total = acc[pl.ds(pl.multiple_of(col * 256, 256), 256), :]
    for d in (1, 3, 2):
        to_x(d).wait_recv()
        total = total + from_x[d - 1]
    p_step(2)
    T[:, 0:256] = total

    @pl.when(moved)
    def _():
        to_leaf().wait()

    T[:, 256:512] = leaf[...].astype(F32)
    corner = remote(T.at[128:256, 0:128], recv.at[0, 128:256, 0:128], l_sem.at[2], l_sem.at[3], partner(0))
    corner.start()
    for k in range(4):
        direct(0, k).start()
        if k < 3:
            r, l = part(k, 1 - c)
            remote(T.at[r, l], recv.at[0, r, l], w_send.at[k], w_recv.at[0, k], partner(0)).start()
    for level in range(1, 7):
        recv[level, 128:256, 0:128] = jnp.zeros((128, 128), F32)
    for h in (0, 1):
        for d in (1, 2, 3):
            near(h, d).wait_send()
            for held in range(4):
                far(h, held, d).wait_send()
    for d in range(4):
        to_core(d).wait_send()
    for d in (1, 2, 3):
        to_x(d).wait_send()
    corner.wait()
    for k in range(3):
        direct(0, k).wait_recv()

    rows = lax.broadcasted_iota(jnp.int32, (256, 256), 0)
    columns = lax.broadcasted_iota(jnp.int32, (256, 256), 1)
    eye = rows == columns

    def level_body(level, carry):
        factor = by_level(level, [0.0] + [2.0 ** (-l / 2.0) for l in range(1, 7)])

        @pl.when(level == 1)
        def _():
            p_step(4)

        @pl.when(level == 2)
        def _():
            p_copy(6).wait()

        @pl.when(level < 2)
        def _():
            p_copy(3 + 2 * level).start()

        s, w = T[:, 0:256], T[:, 256:512]
        cut_other = factor * dot3(p_oth[level], w)
        for k in range(3):
            passed(level, k).wait_recv()
        p = p_own[level]
        cut = dot3(p[:, 0:192], recv[level, 0:192, 256:512])
        direct(level, 3).wait_recv()
        for k in range(4):
            direct(level, k).wait_send()
            if k < 3:
                passed(level, k).wait_send()
        s = s - factor * (cut + dot3(p[:, 192:256], recv[level, 192:256, 256:512]))
        so = recv[level, :, 0:256] - cut_other
        M = jnp.concatenate([s, so], axis=0)
        mt = split(M.T)
        gram = dot3(mt, M)
        cross = dot3(mt, jnp.concatenate([w, recv[level, :, 256:512]], axis=0))
        trace = jnp.sum(jnp.where(eye, gram, 0.0))
        shift = 0.001 * (trace / 256.0 + 1e-6)
        T[:, 0:256] = gram + jnp.where(eye, shift, 0.0)
        T[:, 256:512] = cross
        T[:, 512:768] = jnp.where(eye, 1.0, 0.0)

        def after_block(k):
            @pl.when(level < 6)
            def _():
                direct(level + 1, k).start()
                if k >= 2:
                    direct(level + 1, k - 2).wait_recv()
                    passed(level + 1, k - 2).start()

            if k == 1:

                @pl.when(level < 2)
                def _():
                    p_step(3 + 2 * level)
                    p_copy(4 + 2 * level).start()

        eliminate(T, after_block)
        q = dot3(s, T[:, 512:768], NT)

        @pl.when(level == 0)
        def _():
            leaf_ref[...] = q

        @pl.when(level > 0)
        def _():
            upper_ref[level - 1] = q

        @pl.when(level < 6)
        def _():
            direct(level + 1, 2).wait_recv()
            passed(level + 1, 2).start()

        return carry

    lax.fori_loop(0, 7, level_body, 0)


def whole(front, keep, probes, coupling):
    vmem = pl.BlockSpec(memory_space=pltpu.VMEM)
    dma = pltpu.SemaphoreType.DMA
    return pl.pallas_call(
        whole_kernel,
        out_shape=[
            jax.ShapeDtypeStruct((256, 256), F32),
            jax.ShapeDtypeStruct((6, 256, 256), F32),
        ],
        in_specs=[pl.BlockSpec(memory_space=pl.ANY), vmem, vmem, vmem],
        out_specs=[vmem] * 2,
        scratch_shapes=[
            pltpu.VMEM((2048, 4096), BF),
            pltpu.VMEM((4096, 256), BF),
            pltpu.VMEM((2048, 256), F32),
            pltpu.VMEM((4, 256, 256), F32),
            pltpu.VMEM((3, 256, 256), F32),
            pltpu.VMEM((256, 256), BF),
            pltpu.VMEM((256, 768), F32),
            pltpu.VMEM((7, 256, 512), F32),
            pltpu.VMEM((7, 256, 256), F32),
            pltpu.VMEM((7, 256, 256), F32),
            dma((4,)), dma((2, 3)), dma((2, 3)), dma((2, 4, 3)), dma((2, 4, 3)),
            dma((4,)), dma((4,)), dma((3,)), dma((3,)), dma((4,)),
            dma((4,)), dma((7, 4)), dma((3,)), dma((7, 3)), dma((7,)), dma((7,)),
        ],
        compiler_params=pltpu.CompilerParams(
            collective_id=1, has_side_effects=True, vmem_limit_bytes=52 << 20
        ),
        cost_estimate=pl.CostEstimate(flops=1 << 32, bytes_accessed=1 << 24, transcendentals=0),
    )(front, keep, probes, coupling)


def shards(front, tile_mask, probes, coupling):
    row_index = lax.axis_index("row")
    col_index = lax.axis_index("col")
    tile_above = row_index * 8 + jnp.arange(8, dtype=jnp.int32)
    tile_across = col_index * 16 + jnp.arange(16, dtype=jnp.int32)
    keep = tile_mask * (tile_above[:, None] // 2 != tile_across[None, :] // 2).astype(jnp.int32)
    keep = jnp.repeat(keep.astype(F32), 256, axis=1)
    leaf, upper = whole(front, keep, probes, coupling)
    return leaf, upper


def solution(mesh):
    in_specs = (P("row", "col"), P("row", "col"), P(("col", "row"), None), P(("row", "col"), None))
    out_specs = (P(("row", "col"), None), P(None, ("row", "col"), None))
    return jax.shard_map(shards, mesh=mesh, in_specs=in_specs, out_specs=out_specs, check_vma=False)
```

```python
import jax
import jax.numpy as jnp
from jax import lax
from jax.experimental import pallas as pl
from jax.experimental.pallas import tpu as pltpu
from jax.sharding import PartitionSpec as P

MESH = pl.DeviceIdType.MESH
F32=jnp.float32; BF=jnp.bfloat16

def split(x):
    h=x.astype(BF); l=(x-h.astype(F32)).astype(BF); return h,l
def dg(a,b,dims):
    return lax.dot_general(a,b,(dims,((),())),preferred_element_type=F32)
NN=((1,),(0,)); NT=((1,),(1,)); TN=((0,),(0,))
def dot3(a,b,dims=NN):
    ah,al=a if isinstance(a,tuple) else split(a)
    bh,bl=b if isinstance(b,tuple) else split(b)
    return dg(ah,bh,dims)+(dg(ah,bl,dims)+dg(al,bh,dims))

def lanes(v,c): return jnp.broadcast_to(v[:,c:c+1],(8,128))
def subs(v,i): return jnp.broadcast_to(v[i:i+1,:],(8,128))

def rcp(x):
    return pltpu.reciprocal(x,approx=True)
def factor64(E,off):
    sub=lax.broadcasted_iota(jnp.int32,(8,128),0)
    E=list(E); X=[]
    D=[lanes(E[0],off+j) for j in range(8)]
    for p in range(8):
        V={n:[lanes(E[n],off+8*p+k) for k in range(8)] for n in range(p+1,8)}
        ahead=[lanes(E[p+1],off+8*p+8+j) for j in range(8)] if p<7 else None
        out=None
        for m in range(4):
            P,Q=2*m,2*m+1
            vp,vq=D[P],D[Q]
            aa,bb,cc=subs(vp,P),subs(vq,P),subs(vq,Q)
            r=rcp(aa*cc-bb*bb)
            ep,eq=subs(E[p],P),subs(E[p],Q)
            yp=(cc*ep-bb*eq)*r
            yq=(aa*eq-bb*ep)*r
            zp=(cc*vp-bb*vq)*r
            zq=(aa*vq-bb*vp)*r
            z={j:(subs(zp,j),subs(zq,j)) for j in range(Q+1,8)}
            if m<3:
                mp=jnp.where(sub>Q,vp,0.0); mq=jnp.where(sub>Q,vq,0.0)
                for j in range(Q+1,8):
                    D[j]=D[j]-(mp*z[j][0]+mq*z[j][1])
                E[p]=E[p]-(mp*yp+mq*yq)
            for n in range(p+1,8):
                wp,wq=V[n][P],V[n][Q]
                if n==p+1:
                    tp=(cc*wp-bb*wq)*r
                    tq=(aa*wq-bb*wp)*r
                    for j in range(8):
                        ahead[j]=ahead[j]-(wp*subs(tp,j)+wq*subs(tq,j))
                for j in range(Q+1,8):
                    V[n][j]=V[n][j]-(wp*z[j][0]+wq*z[j][1])
                E[n]=E[n]-(wp*yp+wq*yq)
            ba=bb*rcp(aa)
            sp=lax.rsqrt(aa); sq=lax.rsqrt(cc-bb*ba)
            xp=sp*ep; xq=sq*(eq-ba*ep)
            out=xp if out is None else jnp.where(sub==P,xp,out)
            out=jnp.where(sub==Q,xq,out)
        X.append(out)
        D=ahead
    return X

def eliminate(T, after_block):
    lane = lax.broadcasted_iota(jnp.int32, (8, 128), 1)
    sub = lax.broadcasted_iota(jnp.int32, (8, 128), 0)
    for k in range(4):
        r0 = 64 * k
        off = r0 % 128
        g0 = r0 - off
        E = []
        for p in range(8):
            v = T[r0 + 8 * p : r0 + 8 * p + 8, g0 : g0 + 128]
            inside = (lane >= off) & (lane < off + 64)
            eye = (lane == (64 - off) + 8 * p + sub).astype(F32)
            E.append(jnp.where(inside, v, eye))
        X = jnp.concatenate(factor64(E, off), 0)
        inv = split(X[:, 64 - off : 128 - off])
        block = T[r0 : r0 + 64, :]
        if k < 3:
            Z = dot3(T[r0 + 64 : 256, r0 : r0 + 64], inv, NT)
        Xk = dot3(inv, block)
        rows = lax.broadcasted_iota(jnp.int32, (64, 256), 0) + r0
        columns = lax.broadcasted_iota(jnp.int32, (64, 256), 1)
        T[r0 : r0 + 64, 0:256] = jnp.where(columns >= rows, Xk[:, 0:256], 0.0)
        T[r0 : r0 + 64, 256:512] = Xk[:, 256:512]
        T[r0 : r0 + 64, 512:768] = jnp.where(columns <= rows, Xk[:, 512:768], 0.0)
        after_block(k)
        if k < 3:
            T[r0 + 64 : 256, :] = T[r0 + 64 : 256, :] - dot3(Z, Xk)


def by_level(level, values):
    out = values[-1]
    for i in range(len(values) - 2, -1, -1):
        out = jnp.where(level == i, values[i], out)
    return out


def whole_kernel(front_ref, mask_ref, probes_ref, p_ref, leaf_ref, upper_ref,
                 keep_ref, F, B, acc, from_core, from_x, leaf, T, recv, p_own, p_oth,
                 f_sem, near_send, near_recv, far_send, far_recv, c_send, c_recv, x_send, x_recv, l_sem,
                 d_send, d_recv, w_send, w_recv, p_send, p_recv):
    row, col = lax.axis_index("row"), lax.axis_index("col")
    z, y = row // 4, row % 4
    x, c = col // 2, col % 2
    me = row * 8 + col
    target = col * 16 + row
    source = (me % 16, me // 16)
    moved = target != me

    def at(dz, dy):
        return ((z + dz + 4) % 4 * 4 + (y + dy + 4) % 4, col)

    def along_x(d, other):
        core = 1 - c if other else c
        return (row, (x + d) % 4 * 2 + core)

    def half_rows(dz, dy, h):
        block = (z + dz + 4) % 4 * 4 + (y + dy + 4) % 4
        return pl.ds(pl.multiple_of(block * 256 + h * 128, 128), 128)

    def columns_of(d):
        return pl.ds(pl.multiple_of((z + 4 - d) % 4 * 1024, 1024), 1024)

    def remote(src, dst, send, recv, device):
        return pltpu.make_async_remote_copy(
            src_ref=src, dst_ref=dst, send_sem=send, recv_sem=recv, device_id=device, device_id_type=MESH
        )

    def load(d):
        return pltpu.make_async_copy(front_ref.at[:, columns_of(d)], F.at[:, columns_of(d)], f_sem.at[d])

    def near(h, d):
        r = half_rows(0, 0, h)
        return remote(B.at[r], B.at[r], near_send.at[h, d - 1], near_recv.at[h, d - 1],
                      at(0, d) if h == 0 else at(d, 0))

    def far(h, held, d):
        r = half_rows(0, -held, 0) if h == 0 else half_rows(-held, 0, 1)
        return remote(B.at[r], B.at[r], far_send.at[h, held, d - 1], far_recv.at[h, held, d - 1],
                      at(d, 0) if h == 0 else at(0, d))

    def to_core(d):
        t = pl.ds(pl.multiple_of(((x + d) % 4 * 2 + 1 - c) * 256, 256), 256)
        return remote(acc.at[t], from_core.at[d], c_send.at[d], c_recv.at[d], along_x(0, True))

    def to_x(d):
        t = pl.ds(pl.multiple_of(((x + d) % 4 * 2 + c) * 256, 256), 256)
        return remote(acc.at[t], from_x.at[d - 1], x_send.at[d - 1], x_recv.at[d - 1], along_x(d, False))

    def to_leaf():
        return remote(B.at[own], leaf, l_sem.at[0], l_sem.at[1], (target // 8, target % 8))

    def partner(level):
        h = 2**level if isinstance(level, int) else by_level(level, [1, 2, 4, 8, 16, 32, 64])
        other = me + h * (1 - 2 * ((me // h) % 2))
        return (other // 8, other % 8)

    def p_copy(level):
        return remote(p_own.at[level], p_oth.at[level], p_send.at[level], p_recv.at[level], partner(level))

    def p_step(level):
        p_copy(level).wait()
        p_own[level + 1] = p_own[level] + p_oth[level]

    def part(k, core):
        if k == 3:
            return pl.ds(192, 64), pl.ds(128, 384)
        c0 = 0 if k < 2 else 128
        return pl.ds(pl.multiple_of(64 * k + 32 * core, 32), 32), pl.ds(c0, 512 - c0)

    def direct(level, k):
        r, l = part(k, c)
        return remote(T.at[r, l], recv.at[level, r, l], d_send.at[k], d_recv.at[level, k], partner(level))

    def passed(level, k):
        r, l = part(k, c)
        return remote(recv.at[level, r, l], recv.at[level, r, l], w_send.at[k], w_recv.at[level, k], partner(0))

    order = (0, 1, 3, 2)
    for d in order:
        load(d).start()
    barrier = pltpu.get_barrier_semaphore()
    peers = [at(d, 0) for d in (1, 2, 3)] + [at(0, d) for d in (1, 2, 3)]
    peers += [along_x(d, False) for d in (1, 2, 3)] + [along_x(0, True)]
    for peer in peers:
        pl.semaphore_signal(barrier, inc=1, device_id=peer, device_id_type=MESH)
    pl.semaphore_signal(barrier, inc=1, device_id=source, device_id_type=MESH)

    own = pl.ds(pl.multiple_of(row * 256, 256), 256)
    fetch_probes = pltpu.make_async_copy(probes_ref, B.at[own], l_sem.at[4])
    fetch_p = pltpu.make_async_copy(p_ref, p_own.at[0], l_sem.at[5])
    fetch_probes.start()
    fetch_p.start()
    above = row * 8 + lax.broadcasted_iota(jnp.int32, (8, 16), 0)
    across = col * 16 + lax.broadcasted_iota(jnp.int32, (8, 16), 1)
    kept = jnp.where(above // 2 == across // 2, 0.0, mask_ref[...].astype(F32)).astype(BF)
    spread = lax.broadcasted_iota(jnp.int32, (16, 4096), 1) // 256 == lax.broadcasted_iota(
        jnp.int32, (16, 4096), 0
    )
    keep_ref[...] = jnp.dot(kept, spread.astype(BF), preferred_element_type=F32)
    fetch_probes.wait()
    pl.semaphore_wait(barrier, 11)

    for d in (1, 3, 2):
        near(0, d).start()
        near(1, d).start()
    for d in (1, 3, 2):
        far(0, 0, d).start()
        far(1, 0, d).start()
    fetch_p.wait()
    p_copy(0).start()
    for held in (1, 3, 2):
        near(0, held).wait_recv()
        near(1, held).wait_recv()
        for d in (1, 3, 2):
            far(0, held, d).start()
            far(1, held, d).start()

    @pl.when(moved)
    def _():
        to_leaf().start()

    @pl.when(jnp.logical_not(moved))
    def _():
        leaf[...] = B[own, :]

    p_step(0)
    p_copy(1).start()

    def product(a, d):
        r = pl.ds(pl.multiple_of(a * 256, 256), 256)
        k = keep_ref[pl.ds(a, 1), columns_of(d)].astype(BF)
        return jnp.dot(F[r, columns_of(d)] * k, B[columns_of(d), :], preferred_element_type=F32)

    for d in order:
        load(d).wait()
        if d == 0:
            for e in (1, 2, 3):
                far(1, 0, e).wait_recv()
        else:
            for e in range(4):
                far(0, e, d).wait_recv()
            for e in (1, 2, 3):
                far(1, d, e).wait_recv()
        if d != order[-1]:

            def body(a, carry):
                r = pl.ds(pl.multiple_of(a * 256, 256), 256)
                p = product(a, d)
                acc[r, :] = p if d == 0 else acc[r, :] + p
                return carry

            lax.fori_loop(0, 8, body, 0)
            if d == order[1]:
                p_step(1)
                p_copy(2).start()

    def finish(e):
        to_core(e).wait_recv()
        r = pl.ds(pl.multiple_of(((x + e) % 4 * 2 + c) * 256, 256), 256)
        acc[r, :] = acc[r, :] + from_core[e]
        if e:
            to_x(e).start()

    ahead = None
    for e in (2, 1, 3, 0):
        for other in (True, False):
            a = (x + e) % 4 * 2 + (1 - c if other else c)
            r = pl.ds(pl.multiple_of(a * 256, 256), 256)
            acc[r, :] = acc[r, :] + product(a, order[-1])
            if other:
                to_core(e).start()
        if ahead is not None:
            finish(ahead)
        ahead = e
    finish(0)
    total = acc[pl.ds(pl.multiple_of(col * 256, 256), 256), :]
    for d in (1, 3, 2):
        to_x(d).wait_recv()
        total = total + from_x[d - 1]
    p_step(2)
    T[:, 0:256] = total

    @pl.when(moved)
    def _():
        to_leaf().wait()

    T[:, 256:512] = leaf[...].astype(F32)
    corner = remote(T.at[128:256, 0:128], recv.at[0, 128:256, 0:128], l_sem.at[2], l_sem.at[3], partner(0))
    corner.start()
    for k in range(4):
        direct(0, k).start()
        if k < 3:
            r, l = part(k, 1 - c)
            remote(T.at[r, l], recv.at[0, r, l], w_send.at[k], w_recv.at[0, k], partner(0)).start()
    for level in range(1, 7):
        recv[level, 128:256, 0:128] = jnp.zeros((128, 128), F32)
    for h in (0, 1):
        for d in (1, 2, 3):
            near(h, d).wait_send()
            for held in range(4):
                far(h, held, d).wait_send()
    for d in range(4):
        to_core(d).wait_send()
    for d in (1, 2, 3):
        to_x(d).wait_send()
    corner.wait()
    for k in range(3):
        direct(0, k).wait_recv()

    rows = lax.broadcasted_iota(jnp.int32, (256, 256), 0)
    columns = lax.broadcasted_iota(jnp.int32, (256, 256), 1)
    eye = rows == columns

    def level_body(level, early, last):
        factor = by_level(level, [0.0] + [2.0 ** (-l / 2.0) for l in range(1, 7)])
        s, w = T[:, 0:256], T[:, 256:512]
        cut_other = factor * dot3(p_oth[level], w)
        for k in range(3):
            passed(level, k).wait_recv()
        p = p_own[level]
        cut = dot3(p[:, 0:192], recv[level, 0:192, 256:512])
        direct(level, 3).wait_recv()
        for k in range(4):
            direct(level, k).wait_send()
            if k < 3:
                passed(level, k).wait_send()
        s = s - factor * (cut + dot3(p[:, 192:256], recv[level, 192:256, 256:512]))
        so = recv[level, :, 0:256] - cut_other
        M = jnp.concatenate([s, so], axis=0)
        mt = split(M.T)
        gram = dot3(mt, M)
        cross = dot3(mt, jnp.concatenate([w, recv[level, :, 256:512]], axis=0))
        trace = jnp.sum(jnp.where(eye, gram, 0.0))
        shift = 0.001 * (trace / 256.0 + 1e-6)
        T[:, 0:256] = gram + jnp.where(eye, shift, 0.0)
        T[:, 256:512] = cross
        T[:, 512:768] = jnp.where(eye, 1.0, 0.0)

        def after_block(k):
            if not last:
                direct(level + 1, k).start()
                if k >= 2:
                    direct(level + 1, k - 2).wait_recv()
                    passed(level + 1, k - 2).start()
            if early and k == 1:
                p_step(3 + 2 * level)
                p_copy(4 + 2 * level).start()

        eliminate(T, after_block)
        q = dot3(s, T[:, 512:768], NT)

        if early:

            @pl.when(level == 0)
            def _():
                leaf_ref[...] = q

            @pl.when(level > 0)
            def _():
                upper_ref[0] = q
        else:
            upper_ref[level - 1] = q
        if not last:
            direct(level + 1, 2).wait_recv()
            passed(level + 1, 2).start()
        if early:
            p_step(4 + 2 * level)

            @pl.when(level == 0)
            def _():
                p_copy(5).start()

    p_copy(3).start()

    @pl.loop(0, 2)
    def _(level):
        level_body(level, True, False)

    @pl.loop(2, 6)
    def _(level):
        level_body(level, False, False)

    level_body(6, False, True)


def whole(front, mask, probes, coupling):
    vmem = pl.BlockSpec(memory_space=pltpu.VMEM)
    anywhere = pl.BlockSpec(memory_space=pltpu.HBM)
    dma = pltpu.SemaphoreType.DMA
    return pl.pallas_call(
        whole_kernel,
        out_shape=[
            jax.ShapeDtypeStruct((256, 256), F32),
            jax.ShapeDtypeStruct((6, 256, 256), F32),
        ],
        in_specs=[anywhere, vmem, anywhere, anywhere],
        out_specs=[vmem] * 2,
        scratch_shapes=[
            pltpu.VMEM((8, 4096), F32),
            pltpu.VMEM((2048, 4096), BF),
            pltpu.VMEM((4096, 256), BF),
            pltpu.VMEM((2048, 256), F32),
            pltpu.VMEM((4, 256, 256), F32),
            pltpu.VMEM((3, 256, 256), F32),
            pltpu.VMEM((256, 256), BF),
            pltpu.VMEM((256, 768), F32),
            pltpu.VMEM((7, 256, 512), F32),
            pltpu.VMEM((8, 256, 256), F32),
            pltpu.VMEM((7, 256, 256), F32),
            dma((4,)), dma((2, 3)), dma((2, 3)), dma((2, 4, 3)), dma((2, 4, 3)),
            dma((4,)), dma((4,)), dma((3,)), dma((3,)), dma((6,)),
            dma((4,)), dma((7, 4)), dma((3,)), dma((7, 3)), dma((7,)), dma((7,)),
        ],
        compiler_params=pltpu.CompilerParams(
            collective_id=1, has_side_effects=True, vmem_limit_bytes=40 << 20
        ),
        cost_estimate=pl.CostEstimate(flops=1 << 32, bytes_accessed=1 << 24, transcendentals=0),
    )(front, mask, probes, coupling)


def shards(front, tile_mask, probes, coupling):
    leaf, upper = whole(front, tile_mask, probes, coupling)
    return leaf, upper


def solution(mesh):
    in_specs = (P("row", "col"), P("row", "col"), P(("col", "row"), None), P(("row", "col"), None))
    out_specs = (P(("row", "col"), None), P(None, ("row", "col"), None))
    return jax.shard_map(shards, mesh=mesh, in_specs=in_specs, out_specs=out_specs, check_vma=False)
```

```python
import jax
import jax.numpy as jnp
from jax import lax
from jax.experimental import pallas as pl
from jax.experimental.pallas import tpu as pltpu
from jax.sharding import PartitionSpec as P

MESH = pl.DeviceIdType.MESH
F32=jnp.float32; BF=jnp.bfloat16

def split(x):
    h=x.astype(BF); l=(x-h.astype(F32)).astype(BF); return h,l
def dg(a,b,dims):
    return lax.dot_general(a,b,(dims,((),())),preferred_element_type=F32)
NN=((1,),(0,)); NT=((1,),(1,)); TN=((0,),(0,))
def dot3(a,b,dims=NN):
    ah,al=a if isinstance(a,tuple) else split(a)
    bh,bl=b if isinstance(b,tuple) else split(b)
    return dg(ah,bh,dims)+(dg(ah,bl,dims)+dg(al,bh,dims))

def lanes(v,c): return jnp.broadcast_to(v[:,c:c+1],(8,128))
def subs(v,i): return jnp.broadcast_to(v[i:i+1,:],(8,128))

def rcp(x):
    return pltpu.reciprocal(x,approx=True)
def factor64(E,off):
    sub=lax.broadcasted_iota(jnp.int32,(8,128),0)
    E=list(E); X=[]
    D=[lanes(E[0],off+j) for j in range(8)]
    for p in range(8):
        V={n:[lanes(E[n],off+8*p+k) for k in range(8)] for n in range(p+1,8)}
        ahead=[lanes(E[p+1],off+8*p+8+j) for j in range(8)] if p<7 else None
        out=None
        for m in range(4):
            P,Q=2*m,2*m+1
            vp,vq=D[P],D[Q]
            aa,bb,cc=subs(vp,P),subs(vq,P),subs(vq,Q)
            r=rcp(aa*cc-bb*bb)
            ep,eq=subs(E[p],P),subs(E[p],Q)
            yp=(cc*ep-bb*eq)*r
            yq=(aa*eq-bb*ep)*r
            zp=(cc*vp-bb*vq)*r
            zq=(aa*vq-bb*vp)*r
            z={j:(subs(zp,j),subs(zq,j)) for j in range(Q+1,8)}
            if m<3:
                mp=jnp.where(sub>Q,vp,0.0); mq=jnp.where(sub>Q,vq,0.0)
                for j in range(Q+1,8):
                    D[j]=D[j]-(mp*z[j][0]+mq*z[j][1])
                E[p]=E[p]-(mp*yp+mq*yq)
            for n in range(p+1,8):
                wp,wq=V[n][P],V[n][Q]
                if n==p+1:
                    tp=(cc*wp-bb*wq)*r
                    tq=(aa*wq-bb*wp)*r
                    for j in range(8):
                        ahead[j]=ahead[j]-(wp*subs(tp,j)+wq*subs(tq,j))
                for j in range(Q+1,8):
                    V[n][j]=V[n][j]-(wp*z[j][0]+wq*z[j][1])
                E[n]=E[n]-(wp*yp+wq*yq)
            ba=bb*rcp(aa)
            sp=lax.rsqrt(aa); sq=lax.rsqrt(cc-bb*ba)
            xp=sp*ep; xq=sq*(eq-ba*ep)
            out=xp if out is None else jnp.where(sub==P,xp,out)
            out=jnp.where(sub==Q,xq,out)
        X.append(out)
        D=ahead
    return X

def eliminate(T, after_block):
    lane = lax.broadcasted_iota(jnp.int32, (8, 128), 1)
    sub = lax.broadcasted_iota(jnp.int32, (8, 128), 0)
    for k in range(4):
        r0 = 64 * k
        off = r0 % 128
        g0 = r0 - off
        E = []
        for p in range(8):
            v = T[r0 + 8 * p : r0 + 8 * p + 8, g0 : g0 + 128]
            inside = (lane >= off) & (lane < off + 64)
            eye = (lane == (64 - off) + 8 * p + sub).astype(F32)
            E.append(jnp.where(inside, v, eye))
        X = jnp.concatenate(factor64(E, off), 0)
        inv = split(X[:, 64 - off : 128 - off])
        block = T[r0 : r0 + 64, :]
        if k < 3:
            Z = dot3(T[r0 + 64 : 256, r0 : r0 + 64], inv, NT)
        Xk = dot3(inv, block)
        rows = lax.broadcasted_iota(jnp.int32, (64, 256), 0) + r0
        columns = lax.broadcasted_iota(jnp.int32, (64, 256), 1)
        T[r0 : r0 + 64, 0:256] = jnp.where(columns >= rows, Xk[:, 0:256], 0.0)
        T[r0 : r0 + 64, 256:512] = Xk[:, 256:512]
        T[r0 : r0 + 64, 512:768] = jnp.where(columns <= rows, Xk[:, 512:768], 0.0)
        after_block(k)
        if k < 3:
            T[r0 + 64 : 256, :] = T[r0 + 64 : 256, :] - dot3(Z, Xk)


def by_level(level, values):
    out = values[-1]
    for i in range(len(values) - 2, -1, -1):
        out = jnp.where(level == i, values[i], out)
    return out


def whole_kernel(front_ref, mask_ref, probes_ref, p_ref, leaf_ref, upper_ref,
                 keep_ref, F, B, acc, from_core, from_x, relayed, leaf, T, recv, p_own, p_oth,
                 f_sem, near_send, near_recv, far_send, far_recv, c_send, c_recv, x_send, x_recv, r_send, r_recv, l_sem,
                 d_send, d_recv, w_send, w_recv, p_send, p_recv):
    row, col = lax.axis_index("row"), lax.axis_index("col")
    z, y = row // 4, row % 4
    x, c = col // 2, col % 2
    me = row * 8 + col
    target = col * 16 + row
    source = (me % 16, me // 16)
    moved = target != me

    def at(dz, dy):
        return ((z + dz + 4) % 4 * 4 + (y + dy + 4) % 4, col)

    def along_x(d, other):
        core = 1 - c if other else c
        return (row, (x + d) % 4 * 2 + core)

    def half_rows(dz, dy, h):
        block = (z + dz + 4) % 4 * 4 + (y + dy + 4) % 4
        return pl.ds(pl.multiple_of(block * 256 + h * 128, 128), 128)

    def columns_of(d):
        return pl.ds(pl.multiple_of((z + 4 - d) % 4 * 1024, 1024), 1024)

    def remote(src, dst, send, recv, device):
        return pltpu.make_async_remote_copy(
            src_ref=src, dst_ref=dst, send_sem=send, recv_sem=recv, device_id=device, device_id_type=MESH
        )

    def load(d):
        return pltpu.make_async_copy(front_ref.at[:, columns_of(d)], F.at[:, columns_of(d)], f_sem.at[d])

    def near(h, d):
        r = half_rows(0, 0, h)
        return remote(B.at[r], B.at[r], near_send.at[h, d - 1], near_recv.at[h, d - 1],
                      at(0, d) if h == 0 else at(d, 0))

    def far(h, held, d):
        r = half_rows(0, -held, 0) if h == 0 else half_rows(-held, 0, 1)
        return remote(B.at[r], B.at[r], far_send.at[h, held, d - 1], far_recv.at[h, held, d - 1],
                      at(d, 0) if h == 0 else at(0, d))

    def to_core(d):
        t = pl.ds(pl.multiple_of(((x + d) % 4 * 2 + 1 - c) * 256, 256), 256)
        return remote(acc.at[t], from_core.at[d], c_send.at[d], c_recv.at[d], along_x(0, True))

    def tile_rows(d, h):
        return pl.ds(pl.multiple_of(((x + d) % 4 * 2 + c) * 256 + h * 128, 128), 128)

    def relay(d):
        i = 0 if d == 1 else 1
        return remote(acc.at[tile_rows(2, 1 - i)], relayed.at[i], r_send.at[i], r_recv.at[i], along_x(d, False))

    def to_x(d, h):
        i = 0 if d == 1 else 1
        return remote(acc.at[tile_rows(d, h)], from_x.at[i, pl.ds(h * 128, 128)],
                      x_send.at[i, h], x_recv.at[i, h], along_x(d, False))

    def to_leaf():
        return remote(B.at[own], leaf, l_sem.at[0], l_sem.at[1], (target // 8, target % 8))

    def partner(level):
        h = 2**level if isinstance(level, int) else by_level(level, [1, 2, 4, 8, 16, 32, 64])
        other = me + h * (1 - 2 * ((me // h) % 2))
        return (other // 8, other % 8)

    def p_copy(level):
        return remote(p_own.at[level], p_oth.at[level], p_send.at[level], p_recv.at[level], partner(level))

    def p_step(level):
        p_copy(level).wait()
        p_own[level + 1] = p_own[level] + p_oth[level]

    def part(k, core):
        if k == 3:
            return pl.ds(192, 64), pl.ds(128, 384)
        c0 = 0 if k < 2 else 128
        return pl.ds(pl.multiple_of(64 * k + 32 * core, 32), 32), pl.ds(c0, 512 - c0)

    def direct(level, k):
        r, l = part(k, c)
        return remote(T.at[r, l], recv.at[level, r, l], d_send.at[k], d_recv.at[level, k], partner(level))

    def passed(level, k):
        r, l = part(k, c)
        return remote(recv.at[level, r, l], recv.at[level, r, l], w_send.at[k], w_recv.at[level, k], partner(0))

    order = (0, 1, 3, 2)
    for d in order:
        load(d).start()
    barrier = pltpu.get_barrier_semaphore()
    peers = [at(d, 0) for d in (1, 2, 3)] + [at(0, d) for d in (1, 2, 3)]
    peers += [along_x(d, False) for d in (1, 2, 3)] + [along_x(0, True)]
    for peer in peers:
        pl.semaphore_signal(barrier, inc=1, device_id=peer, device_id_type=MESH)
    pl.semaphore_signal(barrier, inc=1, device_id=source, device_id_type=MESH)

    own = pl.ds(pl.multiple_of(row * 256, 256), 256)
    fetch_probes = pltpu.make_async_copy(probes_ref, B.at[own], l_sem.at[4])
    fetch_p = pltpu.make_async_copy(p_ref, p_own.at[0], l_sem.at[5])
    fetch_probes.start()
    fetch_p.start()
    above = row * 8 + lax.broadcasted_iota(jnp.int32, (8, 16), 0)
    across = col * 16 + lax.broadcasted_iota(jnp.int32, (8, 16), 1)
    kept = jnp.where(above // 2 == across // 2, 0.0, mask_ref[...].astype(F32)).astype(BF)
    spread = lax.broadcasted_iota(jnp.int32, (16, 4096), 1) // 256 == lax.broadcasted_iota(
        jnp.int32, (16, 4096), 0
    )
    keep_ref[...] = jnp.dot(kept, spread.astype(BF), preferred_element_type=F32)
    fetch_probes.wait()
    pl.semaphore_wait(barrier, 11)

    for d in (1, 3, 2):
        near(0, d).start()
        near(1, d).start()
    for d in (1, 3, 2):
        far(0, 0, d).start()
        far(1, 0, d).start()
    fetch_p.wait()
    p_copy(0).start()
    for held in (1, 3, 2):
        near(0, held).wait_recv()
        near(1, held).wait_recv()
        for d in (1, 3, 2):
            far(0, held, d).start()
            far(1, held, d).start()

    @pl.when(moved)
    def _():
        to_leaf().start()

    @pl.when(jnp.logical_not(moved))
    def _():
        leaf[...] = B[own, :]

    p_step(0)
    p_copy(1).start()

    def product(a, d):
        r = pl.ds(pl.multiple_of(a * 256, 256), 256)
        k = keep_ref[pl.ds(a, 1), columns_of(d)].astype(BF)
        return jnp.dot(F[r, columns_of(d)] * k, B[columns_of(d), :], preferred_element_type=F32)

    for d in order:
        load(d).wait()
        if d == 0:
            for e in (1, 2, 3):
                far(1, 0, e).wait_recv()
        else:
            for e in range(4):
                far(0, e, d).wait_recv()
            for e in (1, 2, 3):
                far(1, d, e).wait_recv()
        if d != order[-1]:

            def body(a, carry):
                r = pl.ds(pl.multiple_of(a * 256, 256), 256)
                p = product(a, d)
                acc[r, :] = p if d == 0 else acc[r, :] + p
                return carry

            lax.fori_loop(0, 8, body, 0)
            if d == order[1]:
                p_step(1)
                p_copy(2).start()

    def finish(e):
        to_core(e).wait_recv()
        r = pl.ds(pl.multiple_of(((x + e) % 4 * 2 + c) * 256, 256), 256)
        acc[r, :] = acc[r, :] + from_core[e]
        if e == 2:
            relay(1).start()
            relay(3).start()
        elif e:
            to_x(e, 0 if e == 1 else 1).start()

    ahead = None
    for e in (2, 1, 3, 0):
        for other in (True, False):
            a = (x + e) % 4 * 2 + (1 - c if other else c)
            r = pl.ds(pl.multiple_of(a * 256, 256), 256)
            acc[r, :] = acc[r, :] + product(a, order[-1])
            if other:
                to_core(e).start()
        if ahead is not None:
            finish(ahead)
        ahead = e
    finish(0)
    for d, h, i in ((1, 1, 0), (3, 0, 1)):
        relay(d).wait_recv()
        r = tile_rows(d, h)
        acc[r, :] = acc[r, :] + relayed[i]
        to_x(d, h).start()
    for d, h in ((1, 0), (3, 1), (1, 1), (3, 0)):
        to_x(d, h).wait_recv()
    total = acc[pl.ds(pl.multiple_of(col * 256, 256), 256), :] + (from_x[0] + from_x[1])
    p_step(2)
    T[:, 0:256] = total

    @pl.when(moved)
    def _():
        to_leaf().wait()

    T[:, 256:512] = leaf[...].astype(F32)
    corner = remote(T.at[128:256, 0:128], recv.at[0, 128:256, 0:128], l_sem.at[2], l_sem.at[3], partner(0))
    corner.start()
    for k in range(4):
        direct(0, k).start()
        if k < 3:
            r, l = part(k, 1 - c)
            remote(T.at[r, l], recv.at[0, r, l], w_send.at[k], w_recv.at[0, k], partner(0)).start()
    for level in range(1, 7):
        recv[level, 128:256, 0:128] = jnp.zeros((128, 128), F32)
    for h in (0, 1):
        for d in (1, 2, 3):
            near(h, d).wait_send()
            for held in range(4):
                far(h, held, d).wait_send()
    for d in range(4):
        to_core(d).wait_send()
    for d in (1, 3):
        relay(d).wait_send()
        to_x(d, 0).wait_send()
        to_x(d, 1).wait_send()
    corner.wait()
    for k in range(3):
        direct(0, k).wait_recv()

    rows = lax.broadcasted_iota(jnp.int32, (256, 256), 0)
    columns = lax.broadcasted_iota(jnp.int32, (256, 256), 1)
    eye = rows == columns

    def level_body(level, early, last):
        factor = by_level(level, [0.0] + [2.0 ** (-l / 2.0) for l in range(1, 7)])
        s, w = T[:, 0:256], T[:, 256:512]
        cut_other = factor * dot3(p_oth[level], w)
        for k in range(3):
            passed(level, k).wait_recv()
        p = p_own[level]
        cut = dot3(p[:, 0:192], recv[level, 0:192, 256:512])
        direct(level, 3).wait_recv()
        for k in range(4):
            direct(level, k).wait_send()
            if k < 3:
                passed(level, k).wait_send()
        s = s - factor * (cut + dot3(p[:, 192:256], recv[level, 192:256, 256:512]))
        so = recv[level, :, 0:256] - cut_other
        M = jnp.concatenate([s, so], axis=0)
        mt = split(M.T)
        gram = dot3(mt, M)
        cross = dot3(mt, jnp.concatenate([w, recv[level, :, 256:512]], axis=0))
        trace = jnp.sum(jnp.where(eye, gram, 0.0))
        shift = 0.001 * (trace / 256.0 + 1e-6)
        T[:, 0:256] = gram + jnp.where(eye, shift, 0.0)
        T[:, 256:512] = cross
        T[:, 512:768] = jnp.where(eye, 1.0, 0.0)

        def after_block(k):
            if not last:
                direct(level + 1, k).start()
                if k >= 2:
                    direct(level + 1, k - 2).wait_recv()
                    passed(level + 1, k - 2).start()
            if early and k == 1:
                p_step(3 + 2 * level)
                p_copy(4 + 2 * level).start()

        eliminate(T, after_block)
        q = dot3(s, T[:, 512:768], NT)

        if early:

            @pl.when(level == 0)
            def _():
                leaf_ref[...] = q

            @pl.when(level > 0)
            def _():
                upper_ref[0] = q
        else:
            upper_ref[level - 1] = q
        if not last:
            direct(level + 1, 2).wait_recv()
            passed(level + 1, 2).start()
        if early:
            p_step(4 + 2 * level)

            @pl.when(level == 0)
            def _():
                p_copy(5).start()

    p_copy(3).start()

    @pl.loop(0, 2)
    def _(level):
        level_body(level, True, False)

    @pl.loop(2, 6)
    def _(level):
        level_body(level, False, False)

    level_body(6, False, True)


def whole(front, mask, probes, coupling):
    vmem = pl.BlockSpec(memory_space=pltpu.VMEM)
    anywhere = pl.BlockSpec(memory_space=pltpu.HBM)
    dma = pltpu.SemaphoreType.DMA
    return pl.pallas_call(
        whole_kernel,
        out_shape=[
            jax.ShapeDtypeStruct((256, 256), F32),
            jax.ShapeDtypeStruct((6, 256, 256), F32),
        ],
        in_specs=[anywhere, vmem, anywhere, anywhere],
        out_specs=[vmem] * 2,
        scratch_shapes=[
            pltpu.VMEM((8, 4096), F32),
            pltpu.VMEM((2048, 4096), BF),
            pltpu.VMEM((4096, 256), BF),
            pltpu.VMEM((2048, 256), F32),
            pltpu.VMEM((4, 256, 256), F32),
            pltpu.VMEM((2, 256, 256), F32),
            pltpu.VMEM((2, 128, 256), F32),
            pltpu.VMEM((256, 256), BF),
            pltpu.VMEM((256, 768), F32),
            pltpu.VMEM((7, 256, 512), F32),
            pltpu.VMEM((8, 256, 256), F32),
            pltpu.VMEM((7, 256, 256), F32),
            dma((4,)), dma((2, 3)), dma((2, 3)), dma((2, 4, 3)), dma((2, 4, 3)),
            dma((4,)), dma((4,)), dma((2, 2)), dma((2, 2)), dma((2,)), dma((2,)), dma((6,)),
            dma((4,)), dma((7, 4)), dma((3,)), dma((7, 3)), dma((7,)), dma((7,)),
        ],
        compiler_params=pltpu.CompilerParams(
            collective_id=1, has_side_effects=True, vmem_limit_bytes=40 << 20
        ),
        cost_estimate=pl.CostEstimate(flops=1 << 32, bytes_accessed=1 << 24, transcendentals=0),
    )(front, mask, probes, coupling)


def shards(front, tile_mask, probes, coupling):
    leaf, upper = whole(front, tile_mask, probes, coupling)
    return leaf, upper


def solution(mesh):
    in_specs = (P("row", "col"), P("row", "col"), P(("col", "row"), None), P(("row", "col"), None))
    out_specs = (P(("row", "col"), None), P(None, ("row", "col"), None))
    return jax.shard_map(shards, mesh=mesh, in_specs=in_specs, out_specs=out_specs, check_vma=False)
```

```python
import jax
import jax.numpy as jnp
from jax import lax
from jax.experimental import pallas as pl
from jax.experimental.pallas import tpu as pltpu
from jax.sharding import PartitionSpec as P

MESH = pl.DeviceIdType.MESH
F32=jnp.float32; BF=jnp.bfloat16

def split(x):
    h=x.astype(BF); l=(x-h.astype(F32)).astype(BF); return h,l
def dg(a,b,dims):
    return lax.dot_general(a,b,(dims,((),())),preferred_element_type=F32)
NN=((1,),(0,)); NT=((1,),(1,)); TN=((0,),(0,))
def dot3(a,b,dims=NN):
    ah,al=a if isinstance(a,tuple) else split(a)
    bh,bl=b if isinstance(b,tuple) else split(b)
    return dg(ah,bh,dims)+(dg(ah,bl,dims)+dg(al,bh,dims))

def lanes(v,c): return jnp.broadcast_to(v[:,c:c+1],(8,128))
def subs(v,i): return jnp.broadcast_to(v[i:i+1,:],(8,128))

def rcp(x):
    return pltpu.reciprocal(x,approx=True)
def factor64(E,off):
    sub=lax.broadcasted_iota(jnp.int32,(8,128),0)
    E=list(E); X=[]
    D=[lanes(E[0],off+j) for j in range(8)]
    for p in range(8):
        V={n:[lanes(E[n],off+8*p+k) for k in range(8)] for n in range(p+1,8)}
        ahead=[lanes(E[p+1],off+8*p+8+j) for j in range(8)] if p<7 else None
        out=None
        for m in range(4):
            P,Q=2*m,2*m+1
            vp,vq=D[P],D[Q]
            aa,bb,cc=subs(vp,P),subs(vq,P),subs(vq,Q)
            r=rcp(aa*cc-bb*bb)
            ep,eq=subs(E[p],P),subs(E[p],Q)
            yp=(cc*ep-bb*eq)*r
            yq=(aa*eq-bb*ep)*r
            zp=(cc*vp-bb*vq)*r
            zq=(aa*vq-bb*vp)*r
            z={j:(subs(zp,j),subs(zq,j)) for j in range(Q+1,8)}
            if m<3:
                mp=jnp.where(sub>Q,vp,0.0); mq=jnp.where(sub>Q,vq,0.0)
                for j in range(Q+1,8):
                    D[j]=D[j]-(mp*z[j][0]+mq*z[j][1])
                E[p]=E[p]-(mp*yp+mq*yq)
            for n in range(p+1,8):
                wp,wq=V[n][P],V[n][Q]
                if n==p+1:
                    tp=(cc*wp-bb*wq)*r
                    tq=(aa*wq-bb*wp)*r
                    for j in range(8):
                        ahead[j]=ahead[j]-(wp*subs(tp,j)+wq*subs(tq,j))
                for j in range(Q+1,8):
                    V[n][j]=V[n][j]-(wp*z[j][0]+wq*z[j][1])
                E[n]=E[n]-(wp*yp+wq*yq)
            ba=bb*rcp(aa)
            sp=lax.rsqrt(aa); sq=lax.rsqrt(cc-bb*ba)
            xp=sp*ep; xq=sq*(eq-ba*ep)
            out=xp if out is None else jnp.where(sub==P,xp,out)
            out=jnp.where(sub==Q,xq,out)
        X.append(out)
        D=ahead
    return X

def eliminate(T, after_block):
    lane = lax.broadcasted_iota(jnp.int32, (8, 128), 1)
    sub = lax.broadcasted_iota(jnp.int32, (8, 128), 0)
    for k in range(4):
        r0 = 64 * k
        off = r0 % 128
        g0 = r0 - off
        E = []
        for p in range(8):
            v = T[r0 + 8 * p : r0 + 8 * p + 8, g0 : g0 + 128]
            inside = (lane >= off) & (lane < off + 64)
            eye = (lane == (64 - off) + 8 * p + sub).astype(F32)
            E.append(jnp.where(inside, v, eye))
        X = jnp.concatenate(factor64(E, off), 0)
        inv = split(X[:, 64 - off : 128 - off])
        block = T[r0 : r0 + 64, :]
        if k < 3:
            Z = dot3(T[r0 + 64 : 256, r0 : r0 + 64], inv, NT)
        Xk = dot3(inv, block)
        rows = lax.broadcasted_iota(jnp.int32, (64, 256), 0) + r0
        columns = lax.broadcasted_iota(jnp.int32, (64, 256), 1)
        T[r0 : r0 + 64, 0:256] = jnp.where(columns >= rows, Xk[:, 0:256], 0.0)
        T[r0 : r0 + 64, 256:512] = Xk[:, 256:512]
        T[r0 : r0 + 64, 512:768] = jnp.where(columns <= rows, Xk[:, 512:768], 0.0)
        after_block(k)
        if k < 3:
            T[r0 + 64 : 256, :] = T[r0 + 64 : 256, :] - dot3(Z, Xk)


def by_level(level, values):
    out = values[-1]
    for i in range(len(values) - 2, -1, -1):
        out = jnp.where(level == i, values[i], out)
    return out


def whole_kernel(front_ref, mask_ref, probes_ref, p_ref, leaf_ref, upper_ref,
                 keep_ref, F, B, acc, from_core, from_x, relayed, leaf, T, recv, p_own, p_oth,
                 f_sem, near_send, near_recv, far_send, far_recv, c_send, c_recv, x_send, x_recv, r_send, r_recv, l_sem,
                 d_send, d_recv, w_send, w_recv, p_send, p_recv):
    row, col = lax.axis_index("row"), lax.axis_index("col")
    z, y = row // 4, row % 4
    x, c = col // 2, col % 2
    me = row * 8 + col
    target = col * 16 + row
    source = (me % 16, me // 16)
    moved = target != me

    def at(dz, dy):
        return ((z + dz + 4) % 4 * 4 + (y + dy + 4) % 4, col)

    def along_x(d, other):
        core = 1 - c if other else c
        return (row, (x + d) % 4 * 2 + core)

    def half_rows(dz, dy, h):
        block = (z + dz + 4) % 4 * 4 + (y + dy + 4) % 4
        return pl.ds(pl.multiple_of(block * 256 + h * 128, 128), 128)

    def columns_of(d):
        return pl.ds(pl.multiple_of((z + 4 - d) % 4 * 1024, 1024), 1024)

    def remote(src, dst, send, recv, device):
        return pltpu.make_async_remote_copy(
            src_ref=src, dst_ref=dst, send_sem=send, recv_sem=recv, device_id=device, device_id_type=MESH
        )

    def load(d):
        return pltpu.make_async_copy(front_ref.at[:, columns_of(d)], F.at[:, columns_of(d)], f_sem.at[d])

    def near(h, d):
        r = half_rows(0, 0, h)
        return remote(B.at[r], B.at[r], near_send.at[h, d - 1], near_recv.at[h, d - 1],
                      at(0, d) if h == 0 else at(d, 0))

    def far(h, held, d):
        r = half_rows(0, -held, 0) if h == 0 else half_rows(-held, 0, 1)
        return remote(B.at[r], B.at[r], far_send.at[h, held, d - 1], far_recv.at[h, held, d - 1],
                      at(d, 0) if h == 0 else at(0, d))

    def to_core(d):
        t = pl.ds(pl.multiple_of(((x + d) % 4 * 2 + 1 - c) * 256, 256), 256)
        return remote(acc.at[t], from_core.at[d], c_send.at[d], c_recv.at[d], along_x(0, True))

    def tile_rows(d, h):
        return pl.ds(pl.multiple_of(((x + d) % 4 * 2 + c) * 256 + h * 128, 128), 128)

    def relay(d):
        i = 0 if d == 1 else 1
        return remote(acc.at[tile_rows(2, 1 - i)], relayed.at[i], r_send.at[i], r_recv.at[i], along_x(d, False))

    def to_x(d, h):
        i = 0 if d == 1 else 1
        return remote(acc.at[tile_rows(d, h)], from_x.at[i, pl.ds(h * 128, 128)],
                      x_send.at[i, h], x_recv.at[i, h], along_x(d, False))

    def to_leaf():
        return remote(B.at[own], leaf, l_sem.at[0], l_sem.at[1], (target // 8, target % 8))

    def partner(level):
        h = 2**level if isinstance(level, int) else by_level(level, [1, 2, 4, 8, 16, 32, 64])
        other = me + h * (1 - 2 * ((me // h) % 2))
        return (other // 8, other % 8)

    def p_copy(level):
        return remote(p_own.at[level], p_oth.at[level], p_send.at[level], p_recv.at[level], partner(level))

    def p_step(level):
        p_copy(level).wait()
        p_own[level + 1] = p_own[level] + p_oth[level]

    def part(k, core):
        if k == 3:
            return pl.ds(192, 64), pl.ds(128, 384)
        c0 = 0 if k < 2 else 128
        return pl.ds(pl.multiple_of(64 * k + 32 * core, 32), 32), pl.ds(c0, 512 - c0)

    def direct(level, k):
        r, l = part(k, c)
        return remote(T.at[r, l], recv.at[level, r, l], d_send.at[k], d_recv.at[level, k], partner(level))

    def passed(level, k):
        r, l = part(k, c)
        return remote(recv.at[level, r, l], recv.at[level, r, l], w_send.at[k], w_recv.at[level, k], partner(0))

    order = (0, 1, 3, 2)
    for d in order:
        load(d).start()
    barrier = pltpu.get_barrier_semaphore()
    peers = [at(d, 0) for d in (1, 2, 3)] + [at(0, d) for d in (1, 2, 3)]
    peers += [along_x(d, False) for d in (1, 2, 3)] + [along_x(0, True)]
    for peer in peers:
        pl.semaphore_signal(barrier, inc=1, device_id=peer, device_id_type=MESH)
    pl.semaphore_signal(barrier, inc=1, device_id=source, device_id_type=MESH)

    own = pl.ds(pl.multiple_of(row * 256, 256), 256)
    fetch_probes = pltpu.make_async_copy(probes_ref, B.at[own], l_sem.at[4])
    fetch_p = pltpu.make_async_copy(p_ref, p_own.at[0], l_sem.at[5])
    fetch_probes.start()
    fetch_p.start()
    above = row * 8 + lax.broadcasted_iota(jnp.int32, (8, 16), 0)
    across = col * 16 + lax.broadcasted_iota(jnp.int32, (8, 16), 1)
    kept = jnp.where(above // 2 == across // 2, 0.0, mask_ref[...].astype(F32)).astype(BF)
    spread = lax.broadcasted_iota(jnp.int32, (16, 4096), 1) // 256 == lax.broadcasted_iota(
        jnp.int32, (16, 4096), 0
    )
    keep_ref[...] = jnp.dot(kept, spread.astype(BF), preferred_element_type=F32)
    fetch_probes.wait()
    pl.semaphore_wait(barrier, 11)

    for d in (1, 3, 2):
        near(0, d).start()
        near(1, d).start()
    for d in (1, 3, 2):
        far(0, 0, d).start()
        far(1, 0, d).start()
    fetch_p.wait()
    p_copy(0).start()
    for held in (1, 3, 2):
        near(0, held).wait_recv()
        near(1, held).wait_recv()
        for d in (1, 3, 2):
            far(0, held, d).start()
            far(1, held, d).start()

    @pl.when(moved)
    def _():
        to_leaf().start()

    @pl.when(jnp.logical_not(moved))
    def _():
        leaf[...] = B[own, :]

    p_step(0)
    p_copy(1).start()

    def product(a, d):
        r = pl.ds(pl.multiple_of(a * 256, 256), 256)
        k = keep_ref[pl.ds(a, 1), columns_of(d)].astype(BF)
        return jnp.dot(F[r, columns_of(d)] * k, B[columns_of(d), :], preferred_element_type=F32)

    for d in order:
        load(d).wait()
        if d == 0:
            for e in (1, 2, 3):
                far(1, 0, e).wait_recv()
        else:
            for e in range(4):
                far(0, e, d).wait_recv()
            for e in (1, 2, 3):
                far(1, d, e).wait_recv()
        if d != order[-1]:

            def body(a, carry):
                r = pl.ds(pl.multiple_of(a * 256, 256), 256)
                p = product(a, d)
                acc[r, :] = p if d == 0 else acc[r, :] + p
                return carry

            lax.fori_loop(0, 8, body, 0)
            if d == order[1]:
                p_step(1)
                p_copy(2).start()

    def finish(e):
        to_core(e).wait_recv()
        r = pl.ds(pl.multiple_of(((x + e) % 4 * 2 + c) * 256, 256), 256)
        acc[r, :] = acc[r, :] + from_core[e]
        if e == 2:
            relay(1).start()
            relay(3).start()
        elif e:
            to_x(e, 0 if e == 1 else 1).start()

    ahead = None
    for e in (2, 1, 3, 0):
        for other in (True, False):
            a = (x + e) % 4 * 2 + (1 - c if other else c)
            r = pl.ds(pl.multiple_of(a * 256, 256), 256)
            acc[r, :] = acc[r, :] + product(a, order[-1])
            if other:
                to_core(e).start()
        if ahead is not None:
            finish(ahead)
        ahead = e
    finish(0)
    for d, h, i in ((1, 1, 0), (3, 0, 1)):
        relay(d).wait_recv()
        r = tile_rows(d, h)
        acc[r, :] = acc[r, :] + relayed[i]
        to_x(d, h).start()
    for d, h in ((1, 0), (3, 1), (1, 1), (3, 0)):
        to_x(d, h).wait_recv()
    total = acc[pl.ds(pl.multiple_of(col * 256, 256), 256), :] + (from_x[0] + from_x[1])
    p_step(2)
    T[:, 0:256] = total

    @pl.when(moved)
    def _():
        to_leaf().wait()

    T[:, 256:512] = leaf[...].astype(F32)
    corner = remote(T.at[128:256, 0:128], recv.at[0, 128:256, 0:128], l_sem.at[2], l_sem.at[3], partner(0))
    corner.start()
    for k in range(4):
        direct(0, k).start()
        if k < 3:
            r, l = part(k, 1 - c)
            remote(T.at[r, l], recv.at[0, r, l], w_send.at[k], w_recv.at[0, k], partner(0)).start()
    for level in range(1, 7):
        recv[level, 128:256, 0:128] = jnp.zeros((128, 128), F32)
    for h in (0, 1):
        for d in (1, 2, 3):
            near(h, d).wait_send()
            for held in range(4):
                far(h, held, d).wait_send()
    for d in range(4):
        to_core(d).wait_send()
    for d in (1, 3):
        relay(d).wait_send()
        to_x(d, 0).wait_send()
        to_x(d, 1).wait_send()
    corner.wait()
    for k in range(3):
        direct(0, k).wait_recv()

    rows = lax.broadcasted_iota(jnp.int32, (256, 256), 0)
    columns = lax.broadcasted_iota(jnp.int32, (256, 256), 1)
    eye = rows == columns

    def level_body(level, early, last):
        factor = by_level(level, [0.0] + [2.0 ** (-l / 2.0) for l in range(1, 7)])
        s, w = T[:, 0:256], T[:, 256:512]
        cut_other = factor * dot3(p_oth[level], w)
        for k in range(3):
            passed(level, k).wait_recv()
        p = p_own[level]
        cut = dot3(p[:, 0:192], recv[level, 0:192, 256:512])
        for k in range(3):
            direct(level, k).wait_send()
            passed(level, k).wait_send()
        direct(level, 3).wait_recv()
        direct(level, 3).wait_send()
        s = s - factor * (cut + dot3(p[:, 192:256], recv[level, 192:256, 256:512]))
        so = recv[level, :, 0:256] - cut_other
        M = jnp.concatenate([s, so], axis=0)
        mt = split(M.T)
        gram = dot3(mt, M)
        cross = dot3(mt, jnp.concatenate([w, recv[level, :, 256:512]], axis=0))
        trace = jnp.sum(jnp.where(eye, gram, 0.0))
        shift = 0.001 * (trace / 256.0 + 1e-6)
        T[:, 0:256] = gram + jnp.where(eye, shift, 0.0)
        T[:, 256:512] = cross
        T[:, 512:768] = jnp.where(eye, 1.0, 0.0)

        def after_block(k):
            if not last:
                direct(level + 1, k).start()
                if k == 3:
                    for early_k in range(2):
                        direct(level + 1, early_k).wait_recv()
                        passed(level + 1, early_k).start()
            if early and k == 1:
                p_step(3 + 2 * level)
                p_copy(4 + 2 * level).start()

        eliminate(T, after_block)
        q = dot3(s, T[:, 512:768], NT)

        if early:

            @pl.when(level == 0)
            def _():
                leaf_ref[...] = q

            @pl.when(level > 0)
            def _():
                upper_ref[0] = q
        else:
            upper_ref[level - 1] = q
        if not last:
            direct(level + 1, 2).wait_recv()
            passed(level + 1, 2).start()
        if early:
            p_step(4 + 2 * level)

            @pl.when(level == 0)
            def _():
                p_copy(5).start()

    p_copy(3).start()

    @pl.loop(0, 2)
    def _(level):
        level_body(level, True, False)

    @pl.loop(2, 6)
    def _(level):
        level_body(level, False, False)

    level_body(6, False, True)


def whole(front, mask, probes, coupling):
    vmem = pl.BlockSpec(memory_space=pltpu.VMEM)
    anywhere = pl.BlockSpec(memory_space=pltpu.HBM)
    dma = pltpu.SemaphoreType.DMA
    return pl.pallas_call(
        whole_kernel,
        out_shape=[
            jax.ShapeDtypeStruct((256, 256), F32),
            jax.ShapeDtypeStruct((6, 256, 256), F32),
        ],
        in_specs=[anywhere, vmem, anywhere, anywhere],
        out_specs=[vmem] * 2,
        scratch_shapes=[
            pltpu.VMEM((8, 4096), F32),
            pltpu.VMEM((2048, 4096), BF),
            pltpu.VMEM((4096, 256), BF),
            pltpu.VMEM((2048, 256), F32),
            pltpu.VMEM((4, 256, 256), F32),
            pltpu.VMEM((2, 256, 256), F32),
            pltpu.VMEM((2, 128, 256), F32),
            pltpu.VMEM((256, 256), BF),
            pltpu.VMEM((256, 768), F32),
            pltpu.VMEM((7, 256, 512), F32),
            pltpu.VMEM((8, 256, 256), F32),
            pltpu.VMEM((7, 256, 256), F32),
            dma((4,)), dma((2, 3)), dma((2, 3)), dma((2, 4, 3)), dma((2, 4, 3)),
            dma((4,)), dma((4,)), dma((2, 2)), dma((2, 2)), dma((2,)), dma((2,)), dma((6,)),
            dma((4,)), dma((7, 4)), dma((3,)), dma((7, 3)), dma((7,)), dma((7,)),
        ],
        compiler_params=pltpu.CompilerParams(
            collective_id=1, has_side_effects=True, vmem_limit_bytes=40 << 20
        ),
        cost_estimate=pl.CostEstimate(flops=1 << 32, bytes_accessed=1 << 24, transcendentals=0),
    )(front, mask, probes, coupling)


def shards(front, tile_mask, probes, coupling):
    leaf, upper = whole(front, tile_mask, probes, coupling)
    return leaf, upper


def solution(mesh):
    in_specs = (P("row", "col"), P("row", "col"), P(("col", "row"), None), P(("row", "col"), None))
    out_specs = (P(("row", "col"), None), P(None, ("row", "col"), None))
    return jax.shard_map(shards, mesh=mesh, in_specs=in_specs, out_specs=out_specs, check_vma=False)
```
